128 devices in a mesh: space: 32 (over x, z, core), rep: 4 (over y).
Axes of the slice: x: 4, y: 4, z: 4, core: 2. Of those that a mesh axis runs over, the one named last changes fastest.
Arguments:
- features: bfloat16 [4, 32768, 256], P('rep', 'space'), may hold values from -36 to 36
- neighbours: int32 [4, 64, 26], P('rep', 'space'), may hold values from -1 to 63, as said below
- serial_order: int32 [4, 32768], P('rep', 'space'), may hold values from 0 to 32767, as said below
- kernel_weight: bfloat16 [27, 256, 256], replicated, may hold values from -0.078125 to 0.078125
- input_projection: bfloat16 [256, 768], replicated, may hold values from -2.4 to 2.4
- output_projection: bfloat16 [256, 256], replicated, may hold values from -1.5 to 1.5
- cotangent: bfloat16 [4, 32768, 256], P('rep', 'space'), may hold values from -0.625 to 0.625
Outputs:
- encoded: bfloat16 [4, 32768, 256], P('rep', 'space')
- attended: bfloat16 [4, 32768, 256], P('rep', 'space')
- projection_gradient: float32 [256, 256], replicated
The draws below stay inside these ranges and needn't reach their ends.
Inputs may be any that keep to these rules, and one draw needn't show every extreme that they name: neighbours[t, b, n] is the brick of tile t beside brick b at the n-th offset, or -1; brick b lies on index b // 2 of space, and every brick beside it lies on the same index or the one just before or just after; those on the index before are at offsets with p = -1, those after at p = 1. If c is beside b at an offset, b is beside c at the opposite offset. serial_order[t] is a permutation of 0 to 32767; a point goes to index serial_order[t, r] // 1024 of space. One index of space sends at most 48 points to any one index, exactly 48 to some, and every index sends the same number of points to the index k places further along space (counted modulo the axis) for each k.
All inputs are finite; a program needn't handle non-finite values.
Results may differ from the reference program's by a relative error of at most 0.009.
The reference program's roundings to bfloat16 on the way (of `regrouped`, `normed`, `packed`, `weights` and `context`) count: a program that leaves them out, or rounds other values in their place, can miss the bound.
Values may be sent and summed in bfloat16 or wider, within the bound.
A program may use at most 128 MiB of HBM per device.

```python
import math
import jax
import jax.numpy as jnp
from jax import lax

CHANNELS = 256
HEAD_COUNT = 16
PATCH_SIZE = 1024
BRICK_EDGE = 8
DEVICE_BRICKS = 2
TILE_COUNT = 4
TILE_BRICKS = 64
DEVICE_ROWS = 1024
TILE_POINTS = 32768


def shard_cells(shard_key):
    cell_count = 2 * DEVICE_BRICKS
    lower_key, upper_key, rest_key = jax.random.split(shard_key, 3)
    lower_cell = jax.random.randint(lower_key, (), 0, DEVICE_BRICKS)
    upper_cell = DEVICE_BRICKS + jax.random.randint(upper_key, (), 0, DEVICE_BRICKS)
    shuffled = jax.random.permutation(rest_key, cell_count)
    priority = jnp.zeros((cell_count,), jnp.int32).at[shuffled].set(jnp.arange(cell_count, dtype=jnp.int32))
    priority = priority.at[lower_cell].set(-2).at[upper_cell].set(-1)
    picked = jnp.argsort(priority, stable=True)[:DEVICE_BRICKS]
    return jnp.sort(picked).astype(jnp.int32)


def draw_neighbours(key, part):
    spaces = TILE_BRICKS // DEVICE_BRICKS
    row_cells = DEVICE_BRICKS // 2
    chosen = jax.vmap(shard_cells)(jax.random.split(key, TILE_COUNT * spaces)).reshape(TILE_COUNT, spaces, DEVICE_BRICKS)
    shard_ids = jnp.arange(spaces, dtype=jnp.int32)[None, :, None]
    cell_x = 2 * shard_ids + chosen // DEVICE_BRICKS + jnp.zeros_like(chosen)
    cell_y = chosen % DEVICE_BRICKS // 2
    cell_z = chosen % 2
    brick_ids = shard_ids * DEVICE_BRICKS + jnp.arange(DEVICE_BRICKS, dtype=jnp.int32)[None, None, :] + jnp.zeros_like(chosen)
    tile_ids = jnp.broadcast_to(jnp.arange(TILE_COUNT, dtype=jnp.int32)[:, None, None], chosen.shape)
    id_grid = jnp.full((TILE_COUNT, 2 * spaces + 2, row_cells + 2, 4), -1, jnp.int32)
    id_grid = id_grid.at[tile_ids, cell_x + 1, cell_y + 1, cell_z + 1].set(brick_ids)
    columns = []
    for number in range(27):
        if number == 13:
            continue
        columns.append(id_grid[tile_ids, cell_x + number // 9, cell_y + number // 3 % 3, cell_z + number % 3])
    return jnp.stack(columns, axis=-1).reshape(TILE_COUNT, TILE_BRICKS, 26).astype(jnp.int32)


def tile_order(tile_key):
    spaces = TILE_BRICKS // DEVICE_BRICKS
    half_slots = DEVICE_ROWS // spaces
    most_moved = half_slots // 2
    pair_key, move_key, source_key, target_key = jax.random.split(tile_key, 4)
    pairing = jax.random.permutation(pair_key, spaces)
    moved_rows = jax.random.randint(move_key, (spaces // 2,), 0, most_moved + 1).at[0].set(most_moved)
    counts = jnp.zeros((spaces,), jnp.int32)
    counts = counts.at[pairing[0::2]].set(half_slots + moved_rows).at[pairing[1::2]].set(half_slots - moved_rows)
    count_ends = jnp.cumsum(counts)
    row_ranks = jax.vmap(lambda one_key: jax.random.permutation(one_key, DEVICE_ROWS))(jax.random.split(source_key, spaces))
    further = jnp.searchsorted(count_ends, row_ranks, side='right').astype(jnp.int32)
    target_dev = (jnp.arange(spaces, dtype=jnp.int32)[:, None] + further) % spaces
    slot_tables = jax.vmap(lambda one_key: jax.random.permutation(one_key, DEVICE_ROWS))(jax.random.split(target_key, spaces))
    target_slot = slot_tables[target_dev, row_ranks]
    return (target_dev * DEVICE_ROWS + target_slot).reshape(-1).astype(jnp.int32)


def draw_serial_order(key, part):
    return jax.vmap(tile_order)(jax.random.split(key, TILE_COUNT))


def draw_features(key, part):
    shape_all = (TILE_COUNT, TILE_POINTS, CHANNELS)
    draw_key, row_key, column_key = jax.random.split(key, 3)
    row_scale = jnp.exp(jax.random.uniform(row_key, (TILE_COUNT, TILE_POINTS, 1), jnp.float32, math.log(0.3), math.log(3.0)))
    column_scale = jnp.exp(jax.random.uniform(column_key, (1, 1, CHANNELS), jnp.float32, math.log(0.3), math.log(3.0)))
    noise = jnp.clip(jax.random.normal(draw_key, shape_all, jnp.float32), -4.0, 4.0)
    return (noise * row_scale * column_scale).astype(jnp.bfloat16)


def draw_input_projection(key, part):
    base_key = jax.random.fold_in(key, 0)
    noise_key = jax.random.fold_in(key, 2)
    value_key = jax.random.fold_in(key, 3)
    spread = CHANNELS ** (-0.5)
    base = jnp.clip(jax.random.normal(base_key, (CHANNELS, CHANNELS), jnp.float32), -4.0, 4.0) * spread
    noise = jnp.clip(jax.random.normal(noise_key, (CHANNELS, CHANNELS), jnp.float32), -4.0, 4.0) * spread
    queries = base
    keys_part = noise
    values_part = jnp.clip(jax.random.normal(value_key, (CHANNELS, CHANNELS), jnp.float32), -4.0, 4.0) * spread
    return jnp.concatenate([queries, keys_part, values_part], axis=1).astype(jnp.bfloat16)


def levels(rng, dims, cuts, smallest, largest):
    def one(axis_at, blocks):
        draws = jax.random.uniform(jax.random.fold_in(jax.random.fold_in(rng, 6), axis_at), (blocks,), jnp.float32, smallest / len(cuts), largest / len(cuts))
        return jnp.repeat(jnp.exp(draws), dims[axis_at] // blocks).reshape((-1,) + (1,) * (len(dims) - axis_at - 1))

    gain = one(*cuts[0])
    for cut in cuts[1:]:
        gain = gain * one(*cut)
    return gain


def normal_values(stream_key, shape, scale, bound, pieces=(), held_as=jnp.bfloat16):
    array = jax.random.normal(stream_key, shape, jnp.float32) * scale
    if len(pieces) > 0:
        array = levels(stream_key, shape, pieces, -0.22, 0.18) * array
    return jnp.clip(array, min=-bound, max=bound).astype(held_as)


def setup_inputs(seed: int = 0) -> dict:
    splits = jax.random.split(jax.random.key(seed), 8)
    features = draw_features(jax.random.fold_in(splits[7], 71), 0)
    neighbours = draw_neighbours(jax.random.fold_in(splits[7], 71), 0)
    serial_order = draw_serial_order(jax.random.fold_in(splits[7], 71), 0)
    kernel_weight = normal_values(splits[3], (27, CHANNELS, CHANNELS), (27 * CHANNELS) ** -0.5, 0.078125)
    input_projection = draw_input_projection(jax.random.fold_in(splits[7], 71), 0)
    output_projection = normal_values(splits[5], (CHANNELS, CHANNELS), (CHANNELS // 16) ** -0.5, 1.5)
    cotangent = normal_values(splits[6], (TILE_COUNT, TILE_POINTS, CHANNELS), 0.04, 0.625, ((0, 4), (1, 32)))
    return {"features": features, "neighbours": neighbours, "serial_order": serial_order, "kernel_weight": kernel_weight, "input_projection": input_projection, "output_projection": output_projection, "cotangent": cotangent}


KERNEL_STEPS = tuple(((number // 9 - 1, number // 3 % 3 - 1, number % 3 - 1) for number in range(27)))
NEIGHBOUR_STEPS = tuple((offset for offset in KERNEL_STEPS if offset != (0, 0, 0)))

def padded_span(component, extent):
    if component < 0:
        return (0, 1)
    if component > 0:
        return (extent + 1, extent + 2)
    return (1, extent + 1)

def inside_span(component, extent):
    if component < 0:
        return (extent - 1, extent)
    if component > 0:
        return (0, 1)
    return (0, extent)

def build_padded(center, layer_pools, first_ids, neighbour_ids):
    bricks = center.shape[0]
    extent = center.shape[1]
    padded = jnp.zeros((bricks, extent + 2, extent + 2, extent + 2, center.shape[-1]), center.dtype)
    padded = padded.at[:, 1:extent + 1, 1:extent + 1, 1:extent + 1].set(center)
    for number, offset in enumerate(NEIGHBOUR_STEPS):
        target = neighbour_ids[:, number]
        across = inside_span(offset[1], extent)
        upward = inside_span(offset[2], extent)
        source_pool = layer_pools[offset[0] + 1][:, :, across[0]:across[1], upward[0]:upward[1]]
        source = jnp.clip(target - first_ids[offset[0] + 1], 0, source_pool.shape[0] - 1).astype(jnp.int32)
        picked = jnp.take(source_pool, source, axis=0)
        picked = jnp.where((target >= 0)[:, None, None, None, None], picked, jnp.zeros_like(picked))
        regions = [padded_span(component, extent) for component in offset]
        padded = padded.at[:, regions[0][0]:regions[0][1], regions[1][0]:regions[1][1], regions[2][0]:regions[2][1]].set(picked)
    return padded

def convolve(padded, kernel_weight):
    bricks = padded.shape[0]
    extent = padded.shape[1] - 2
    width_in = padded.shape[-1]
    summed = jnp.zeros((bricks * extent ** 3, kernel_weight.shape[2]), jnp.float32)
    for number, offset in enumerate(KERNEL_STEPS):
        window = padded[:, 1 + offset[0]:1 + offset[0] + extent, 1 + offset[1]:1 + offset[1] + extent, 1 + offset[2]:1 + offset[2] + extent]
        summed = summed + jnp.dot(window.reshape(-1, width_in), kernel_weight[number], preferred_element_type=jnp.float32)
    return summed

def layer_norm(rows_in):
    centred = rows_in - lax.optimization_barrier(jnp.mean(rows_in, axis=-1, keepdims=True))
    return centred * lax.rsqrt(lax.optimization_barrier(jnp.mean(centred * centred, axis=-1, keepdims=True)) + 1e-05)

def patch_attention(block):
    head_width = block.shape[-1]
    queries = block[:, 0].astype(jnp.float32)
    keys_in = block[:, 1].astype(jnp.float32)
    values_in = block[:, 2].astype(jnp.float32)
    scores = jnp.einsum('qhd,khd->hqk', queries, keys_in, precision=lax.Precision.HIGHEST) * head_width ** (-0.5)
    highest = lax.optimization_barrier(jnp.max(scores, axis=-1, keepdims=True))
    lifted = jnp.exp(scores - highest)
    weights = (lifted / lax.optimization_barrier(jnp.sum(lifted, axis=-1, keepdims=True))).astype(jnp.bfloat16)
    return jnp.einsum('hqk,khd->qhd', weights.astype(jnp.float32), values_in, precision=lax.Precision.HIGHEST)

def reference(features, neighbours, serial_order, kernel_weight, input_projection, output_projection, cotangent):
    extent = BRICK_EDGE
    head_width = CHANNELS // HEAD_COUNT
    encoded_tiles = []
    attended_tiles = []
    gradient = jnp.zeros((CHANNELS, CHANNELS), jnp.float32)
    for tile_index in range(TILE_COUNT):
        tile_rows = features[tile_index]
        brick_cubes = tile_rows.reshape(TILE_BRICKS, extent, extent, extent, CHANNELS)
        layer_pools = (brick_cubes[:, extent - 1:], brick_cubes, brick_cubes[:, :1])
        padded = build_padded(brick_cubes, layer_pools, (0, 0, 0), neighbours[tile_index])
        encoded = (tile_rows.astype(jnp.float32) + convolve(padded, kernel_weight)).astype(jnp.bfloat16)
        regrouped = jnp.zeros_like(encoded).at[serial_order[tile_index]].set(encoded)
        residual = regrouped.astype(jnp.float32)
        normed = layer_norm(residual).astype(jnp.bfloat16)
        packed = jnp.dot(normed, input_projection, preferred_element_type=jnp.float32).astype(jnp.bfloat16)
        blocks = packed.reshape(TILE_POINTS // PATCH_SIZE, PATCH_SIZE, 3, HEAD_COUNT, head_width)
        context = lax.map(patch_attention, blocks).reshape(TILE_POINTS, CHANNELS).astype(jnp.bfloat16)
        attended = (residual + jnp.dot(context, output_projection, preferred_element_type=jnp.float32)).astype(jnp.bfloat16)
        gradient = gradient + jnp.dot(context.T, cotangent[tile_index], preferred_element_type=jnp.float32)
        encoded_tiles.append(encoded)
        attended_tiles.append(attended)
    return (jnp.stack(encoded_tiles), jnp.stack(attended_tiles), gradient)
```

```python
import functools

import jax
import jax.numpy as jnp
from jax import lax
from jax.experimental import pallas as pl
from jax.experimental.pallas import tpu as pltpu
from jax.sharding import PartitionSpec as P

HEADS = 16
EDGE = 8
MESH = pl.DeviceIdType.MESH
F32 = jnp.float32
BF16 = jnp.bfloat16
VMEM_LIMIT = 60 * 1024 * 1024


def dot(a, b):
    return jnp.dot(a, b, preferred_element_type=F32)


def dot_t(a, b):
    return lax.dot_general(a, b, (((1,), (1,)), ((), ())), preferred_element_type=F32)


def iota(shape, dim):
    return lax.broadcasted_iota(jnp.int32, shape, dim)


def onehot(mask):
    return jnp.where(mask, 1.0, 0.0).astype(BF16)


def front_kernel(
    spaces, cap, feat, nb, order, w_hbm, enc, reg,
    w, x, halo_l, halo_r, table, got, send, recv,
    w_sem, hs, hr, ts, tr, rs, rr,
):
    me = lax.axis_index("space")
    rows, width = feat.shape
    face = EDGE * EDGE
    brick = EDGE * face
    bricks = rows // brick
    load = pltpu.make_async_copy(w_hbm, w, w_sem)
    load.start()

    def peer(k):
        return {"space": lax.rem(me + k, spaces)}

    barrier = pltpu.get_barrier_semaphore()

    def greet(k, carry):
        pl.semaphore_signal(barrier, inc=1, device_id=peer(k), device_id_type=MESH)
        return carry

    lax.fori_loop(1, spaces, greet, 0)

    places = order[...]
    shift = rows.bit_length() - 1
    owner = lax.shift_right_logical(places, shift)
    slot = places & (rows - 1)
    ahead = (owner - me + spaces) & (spaces - 1)
    chosen = jnp.where(iota((spaces, rows), 0) == ahead, 1.0, 0.0)
    before = onehot(iota((rows, rows), 0) < iota((rows, rows), 1))
    rank = jnp.sum(chosen * dot(chosen.astype(BF16), before), axis=0, keepdims=True)
    high = lax.shift_right_logical(slot, 5).astype(F32)
    low = (slot & 31).astype(F32)
    lanes = table.shape[2]
    by_rank = onehot(iota((lanes, rows), 0).astype(F32) == rank)
    stacked = jnp.concatenate([chosen * high, chosen * low, chosen], axis=0).astype(BF16)
    found = dot_t(stacked, by_rank)
    slots = found[:spaces] * 32.0 + found[spaces : 2 * spaces]
    slots = jnp.where(found[2 * spaces :] > 0.5, slots, -1.0)
    table[...] = jnp.broadcast_to(slots[:, None, :], table.shape)
    row_at = ahead.astype(F32) * float(cap) + rank

    pl.semaphore_wait(barrier, spaces - 1)

    halos = []
    for b in range(bricks):
        for source, dst, step, n in (
            (b * brick + brick - face, halo_l, 1, 2 * b),
            (b * brick, halo_r, spaces - 1, 2 * b + 1),
        ):
            copy = pltpu.make_async_remote_copy(
                src_ref=feat.at[pl.ds(source, face)], dst_ref=dst.at[b], send_sem=hs.at[n], recv_sem=hr.at[n],
                device_id=peer(step), device_id_type=MESH,
            )
            copy.start()
            halos.append(copy)

    def table_copy(k):
        return pltpu.make_async_remote_copy(
            src_ref=table.at[k], dst_ref=got.at[k], send_sem=ts.at[k], recv_sem=tr.at[k],
            device_id=peer(k), device_id_type=MESH,
        )

    def row_copy(k):
        return pltpu.make_async_remote_copy(
            src_ref=send.at[k], dst_ref=recv.at[k], send_sem=rs.at[k], recv_sem=rr.at[k],
            device_id=peer(k), device_id_type=MESH,
        )

    def start_table(k, carry):
        table_copy(k).start()
        return carry

    lax.fori_loop(1, spaces, start_table, 0)

    depth = iota((EDGE + 2, EDGE, width), 1)

    def beside(b, offset, source_id):
        p, q, r = offset
        number = 9 * (p + 1) + 3 * (q + 1) + (r + 1)
        number -= number > 13
        target = nb[b, number]
        return jnp.where((target == source_id) & (target >= 0), 1.0, 0.0)

    def layer(ref, first):
        return ref[pl.ds(first, face)].astype(F32).reshape(EDGE, EDGE, width)

    def write_layer(b, i, p, sources, ids, own):
        grown = []
        for r in (-1, 0, 1):
            parts = []
            for q in (-1, 0, 1):
                part = slice(EDGE - 1, EDGE) if q < 0 else slice(0, 1) if q > 0 else slice(0, EDGE)
                if own is not None and q == 0 and r == 0:
                    parts.append(own)
                    continue
                total = None
                for source, one_id in zip(sources, ids):
                    term = source[part] * beside(b, (p, q, r), one_id)
                    total = term if total is None else total + term
                parts.append(total)
            grown.append(jnp.concatenate(parts, axis=0))
        below, here, above = grown
        variants = (
            pltpu.roll(jnp.where(depth == EDGE - 1, below, here), 1, 1),
            here,
            pltpu.roll(jnp.where(depth == 0, above, here), EDGE - 1, 1),
        )
        first = i * face if isinstance(i, int) else pl.multiple_of(i * face, face)
        for q in range(3):
            for r in range(3):
                n = 3 * q + r
                x[b, pl.ds(first, face), n * width : (n + 1) * width] = (
                    variants[r][q : q + EDGE].reshape(face, width).astype(BF16)
                )

    own_ids = [me * bricks + n for n in range(bricks)]
    left_ids = [(me - 1) * bricks + n for n in range(bricks)]
    right_ids = [(me + 1) * bricks + n for n in range(bricks)]

    def inner(i, carry):
        sources = [layer(feat, pl.multiple_of(n * brick + i * face, face)) for n in range(bricks)]
        for b in range(bricks):
            write_layer(b, i + 1, 0, sources, own_ids, sources[b])
        return carry

    lax.fori_loop(0, EDGE, inner, 0)

    for copy in halos:
        copy.wait_recv()
    tops = [layer(feat, n * brick + brick - face) for n in range(bricks)]
    bottoms = [layer(feat, n * brick) for n in range(bricks)]
    lefts = [layer(halo_l.at[n], 0) for n in range(bricks)]
    rights = [layer(halo_r.at[n], 0) for n in range(bricks)]
    for b in range(bricks):
        write_layer(b, 0, -1, lefts + tops, left_ids + own_ids, None)
        write_layer(b, EDGE + 1, 1, bottoms + rights, own_ids + right_ids, None)

    load.wait()
    tile = 256

    def conv(n, carry):
        b, first = n // (brick // tile), n % (brick // tile) * tile
        acc = jnp.zeros((tile, width), F32)
        for p in range(3):
            window = x[b, pl.ds(pl.multiple_of(first + p * face, face), tile), :]
            acc = acc + dot(window, w[9 * p : 9 * p + 9].reshape(9 * width, width))
        at = pl.ds(pl.multiple_of(n * tile, tile), tile)
        enc[at] = (feat[at].astype(F32) + acc).astype(BF16)
        return carry

    lax.fori_loop(0, rows // tile, conv, 0)

    group = 8
    for c in range(spaces // group):
        wanted = (iota((group * cap, rows), 0) + c * group * cap).astype(F32)
        block = dot(onehot(wanted == row_at), enc[...]).astype(BF16)
        send[c * group : (c + 1) * group] = block.reshape(group, cap, width)
        for k in range(max(1, c * group), (c + 1) * group):
            row_copy(k).start()
    recv[0] = send[0]
    got[0] = table[0]

    def wait_table(k, carry):
        table_copy(k).wait()
        return carry

    lax.fori_loop(1, spaces, wait_table, 0)
    total = jnp.zeros((rows, width), F32)
    column = iota((8, 128), 1)
    for c in range(spaces // group):
        for k in range(max(1, c * group), (c + 1) * group):
            row_copy(k).wait_recv()
        blocks = []
        for t in range(c * group * cap // 128, (c + 1) * group * cap // 128):
            lane = jnp.full((8, 128), -1.0, F32)
            for k in range(spaces):
                start, end = max(0, k * cap - 128 * t), min(128, (k + 1) * cap - 128 * t)
                if start >= end:
                    continue
                moved = got[k]
                if (k * cap - 128 * t) % 128:
                    moved = pltpu.roll(moved, (k * cap - 128 * t) % 128, 1)
                lane = jnp.where((column >= start) & (column < end), moved, lane)
            blocks.append(onehot(iota((rows, 128), 0).astype(F32) == lane[0:1]))
        arrived = recv[c * group : (c + 1) * group].reshape(group * cap, width)
        total = total + dot(jnp.concatenate(blocks, axis=1), arrived)
    reg[...] = total.astype(BF16)

    def wait_sent(k, carry):
        row_copy(k).wait_send()
        return carry

    lax.fori_loop(1, spaces, wait_sent, 0)
    for copy in halos:
        copy.wait_send()


def front(features, neighbours, order, weight):
    spaces = lax.axis_size("space")
    rows, width = features.shape
    cap = 3 * rows // (2 * spaces)
    bricks = rows // EDGE**3
    face = EDGE * EDGE
    vmem = pl.BlockSpec(memory_space=pltpu.VMEM)
    return pl.pallas_call(
        functools.partial(front_kernel, spaces, cap),
        out_shape=[jax.ShapeDtypeStruct((rows, width), BF16)] * 2,
        in_specs=[vmem, pl.BlockSpec(memory_space=pltpu.SMEM), vmem, pl.BlockSpec(memory_space=pl.ANY)],
        out_specs=[vmem, vmem],
        scratch_shapes=[
            pltpu.VMEM(weight.shape, BF16),
            pltpu.VMEM((bricks, (EDGE + 2) * face, 9 * width), BF16),
            pltpu.VMEM((bricks, face, width), BF16),
            pltpu.VMEM((bricks, face, width), BF16),
            pltpu.VMEM((spaces, 8, 128), F32),
            pltpu.VMEM((spaces, 8, 128), F32),
            pltpu.VMEM((spaces, cap, width), BF16),
            pltpu.VMEM((spaces, cap, width), BF16),
            pltpu.SemaphoreType.DMA,
            pltpu.SemaphoreType.DMA((2 * bricks,)),
            pltpu.SemaphoreType.DMA((2 * bricks,)),
            pltpu.SemaphoreType.DMA((spaces,)),
            pltpu.SemaphoreType.DMA((spaces,)),
            pltpu.SemaphoreType.DMA((spaces,)),
            pltpu.SemaphoreType.DMA((spaces,)),
        ],
        compiler_params=pltpu.CompilerParams(collective_id=0, has_side_effects=True, vmem_limit_bytes=VMEM_LIMIT),
        cost_estimate=pl.CostEstimate(
            flops=2 * rows * 27 * width * width, bytes_accessed=weight.size * 2 + 6 * rows * width, transcendentals=0
        ),
        name="front",
    )(features, neighbours, order, weight)


def attention_kernel(reg, wi, wo, cot, att, grad, q, k, v, ctx):
    rows, width = reg.shape
    head = width // HEADS
    half = width // 2
    residual = reg[...].astype(F32)
    centred = residual - jnp.mean(residual, axis=-1, keepdims=True)
    variance = jnp.mean(centred * centred, axis=-1, keepdims=True)
    normed = (centred * lax.rsqrt(variance + 1e-05)).astype(BF16)
    packed = dot(normed, wi[...]).astype(BF16)
    q[...] = packed[:, :width] * jnp.asarray(head**-0.5, BF16)
    k[...] = packed[:, width : 2 * width]
    ones = jnp.ones((rows, half), BF16)
    for n in range(2):
        v[n] = jnp.concatenate([packed[:, 2 * width + n * half : 2 * width + (n + 1) * half], ones], axis=1)
    ctx[...] = jnp.zeros_like(ctx)
    tile = 256
    lane_q = iota((tile, width), 1) // head
    lane_c = iota((tile, half), 1) // head

    def one_head(h, carry):
        side = h // (HEADS // 2)
        values = v[side]
        for t in range(rows // tile):
            at = slice(t * tile, (t + 1) * tile)
            queries = jnp.where(lane_q == h, q[at], jnp.zeros((), BF16))
            scores = dot_t(queries, k[...])
            lifted = jnp.exp(scores - jnp.max(scores, axis=-1, keepdims=True))
            both = dot(lifted.astype(BF16), values)
            ratio = both[:, :half] / both[:, half:]
            ctx[side, at] += jnp.where(lane_c == h - side * (HEADS // 2), ratio, 0.0)
        return carry

    lax.fori_loop(0, HEADS, one_head, 0)
    context = jnp.concatenate([ctx[0], ctx[1]], axis=1).astype(BF16)
    att[...] = (residual + dot(context, wo[...])).astype(BF16)
    grad[...] = lax.dot_general(context, cot[...], (((0,), (0,)), ((), ())), preferred_element_type=F32)


def attention(regrouped, wi, wo, cot):
    rows, width = regrouped.shape
    vmem = pl.BlockSpec(memory_space=pltpu.VMEM)
    return pl.pallas_call(
        attention_kernel,
        out_shape=[jax.ShapeDtypeStruct((rows, width), BF16), jax.ShapeDtypeStruct((width, width), F32)],
        in_specs=[vmem] * 4,
        out_specs=[vmem, vmem],
        scratch_shapes=[
            pltpu.VMEM((rows, width), BF16),
            pltpu.VMEM((rows, width), BF16),
            pltpu.VMEM((2, rows, width), BF16),
            pltpu.VMEM((2, rows, width // 2), F32),
        ],
        compiler_params=pltpu.CompilerParams(vmem_limit_bytes=VMEM_LIMIT),
        cost_estimate=pl.CostEstimate(
            flops=4 * HEADS * rows * rows * width, bytes_accessed=8 * rows * width, transcendentals=HEADS * rows * rows
        ),
        name="attention",
    )(regrouped, wi, wo, cot)


def reduce_kernel(spaces, reps, term, out, first, second, part, sum_all, s1, r1, s2, r2, s3, r3, s4, r4):
    space, rep = lax.axis_index("space"), lax.axis_index("rep")
    planes = spaces // 2
    chip, core = space // 2, space % 2
    others = 2 * reps
    place = rep * 2 + core

    def across(n):
        return {"space": lax.rem(chip + n, planes) * 2 + core}

    def along(n):
        there = lax.rem(place + n, others)
        return {"space": chip * 2 + there % 2, "rep": there // 2}

    barrier = pltpu.get_barrier_semaphore()

    def greet_a(n, carry):
        pl.semaphore_signal(barrier, inc=1, device_id=across(n), device_id_type=MESH)
        return carry

    def greet_b(n, carry):
        pl.semaphore_signal(barrier, inc=1, device_id=along(n), device_id_type=MESH)
        return carry

    lax.fori_loop(1, planes, greet_a, 0)
    lax.fori_loop(1, others, greet_b, 0)
    pl.semaphore_wait(barrier, planes + others - 2)

    def copy(src, dst, sems, n, device):
        return pltpu.make_async_remote_copy(
            src_ref=src, dst_ref=dst, send_sem=sems[0].at[n], recv_sem=sems[1].at[n], device_id=device, device_id_type=MESH
        )

    def c1(n):
        there = lax.rem(chip + n, planes)
        return copy(term.at[there], first.at[n], (s1, r1), n, across(n))

    def c2(n):
        there = lax.rem(place + n, others)
        return copy(part.at[there], second.at[n], (s2, r2), n, along(n))

    def c3(n):
        return copy(sum_all.at[chip, place], sum_all.at[chip, place], (s3, r3), n, along(n))

    def w3(n):
        there = lax.rem(place - n + others, others)
        return copy(sum_all.at[chip, there], sum_all.at[chip, there], (s3, r3), n, along(n))

    def c4(n):
        return copy(sum_all.at[chip], sum_all.at[chip], (s4, r4), n, across(n))

    def w4(n):
        there = lax.rem(chip - n + planes, planes)
        return copy(sum_all.at[there], sum_all.at[there], (s4, r4), n, across(n))

    def run(count, make):
        def body(n, carry):
            make(n)
            return carry

        lax.fori_loop(1, count, body, 0)

    run(planes, lambda n: c1(n).start())
    first[0] = term[chip]
    run(planes, lambda n: c1(n).wait())
    part[...] = jnp.sum(first[...], axis=0)
    run(others, lambda n: c2(n).start())
    second[0] = part[place]
    run(others, lambda n: c2(n).wait())
    sum_all[chip, place] = jnp.sum(second[...], axis=0)
    run(others, lambda n: c3(n).start())
    run(others, lambda n: c3(n).wait_send())
    run(others, lambda n: w3(n).wait_recv())
    run(planes, lambda n: c4(n).start())
    run(planes, lambda n: c4(n).wait_send())
    run(planes, lambda n: w4(n).wait_recv())
    out[...] = sum_all[...]


def reduce_all(term):
    spaces, reps = lax.axis_size("space"), lax.axis_size("rep")
    rows, width = term.shape
    planes, others = spaces // 2, 2 * reps
    small = rows // planes // others
    sub = small * width // 128
    shape = (planes, others, sub, 128)
    vmem = pl.BlockSpec(memory_space=pltpu.VMEM)
    out = pl.pallas_call(
        functools.partial(reduce_kernel, spaces, reps),
        out_shape=jax.ShapeDtypeStruct(shape, F32),
        in_specs=[vmem],
        out_specs=vmem,
        scratch_shapes=[
            pltpu.VMEM((planes, others, sub, 128), F32),
            pltpu.VMEM((others, sub, 128), F32),
            pltpu.VMEM((others, sub, 128), F32),
            pltpu.VMEM(shape, F32),
        ]
        + [pltpu.SemaphoreType.DMA((planes,))] * 2
        + [pltpu.SemaphoreType.DMA((others,))] * 4
        + [pltpu.SemaphoreType.DMA((planes,))] * 2,
        compiler_params=pltpu.CompilerParams(collective_id=1, has_side_effects=True),
        name="reduce_all",
    )(term.reshape(shape))
    return out.reshape(rows, width)


def local(features, neighbours, serial_order, kernel_weight, input_projection, output_projection, cotangent):
    encoded, regrouped = front(features[0], neighbours[0], serial_order, kernel_weight)
    attended, term = attention(regrouped, input_projection, output_projection, cotangent[0])
    gradient = reduce_all(term)
    return encoded[None], attended[None], gradient


def solution(mesh):
    in_specs = (
        P("rep", "space", None),
        P("rep", "space", None),
        P("rep", "space"),
        P(),
        P(),
        P(),
        P("rep", "space", None),
    )
    out_specs = (P("rep", "space", None), P("rep", "space", None), P())
    return jax.shard_map(local, mesh=mesh, in_specs=in_specs, out_specs=out_specs, check_vma=False)
```

```python
import functools

import jax
import jax.numpy as jnp
from jax import lax
from jax.experimental import pallas as pl
from jax.experimental.pallas import tpu as pltpu
from jax.sharding import PartitionSpec as P

HEADS = 16
EDGE = 8
MESH = pl.DeviceIdType.MESH
F32 = jnp.float32
BF16 = jnp.bfloat16
VMEM_LIMIT = 60 * 1024 * 1024


def dot(a, b):
    return jnp.dot(a, b, preferred_element_type=F32)


def dot_t(a, b):
    return lax.dot_general(a, b, (((1,), (1,)), ((), ())), preferred_element_type=F32)


def iota(shape, dim):
    return lax.broadcasted_iota(jnp.int32, shape, dim)


def onehot(mask):
    return jnp.where(mask, 1.0, 0.0).astype(BF16)


def front_kernel(
    spaces, cap, feat, nb, order, w_hbm, enc, reg,
    w, x, halo_l, halo_r, table, got, send, recv,
    w_sem, hs, hr, ts, tr, rs, rr,
):
    me = lax.axis_index("space")
    rows, width = feat.shape
    face = EDGE * EDGE
    brick = EDGE * face
    bricks = rows // brick
    load = pltpu.make_async_copy(w_hbm, w, w_sem)
    load.start()

    def peer(k):
        return {"space": lax.rem(me + k, spaces)}

    barrier = pltpu.get_barrier_semaphore()

    def greet(k, carry):
        pl.semaphore_signal(barrier, inc=1, device_id=peer(k), device_id_type=MESH)
        return carry

    lax.fori_loop(1, spaces, greet, 0)

    places = order[...]
    shift = rows.bit_length() - 1
    owner = lax.shift_right_logical(places, shift)
    slot = places & (rows - 1)
    ahead = (owner - me + spaces) & (spaces - 1)
    chosen = jnp.where(iota((spaces, rows), 0) == ahead, 1.0, 0.0)
    before = onehot(iota((rows, rows), 0) < iota((rows, rows), 1))
    rank = jnp.sum(chosen * dot(chosen.astype(BF16), before), axis=0, keepdims=True)
    high = lax.shift_right_logical(slot, 5).astype(F32)
    low = (slot & 31).astype(F32)
    lanes = table.shape[2]
    by_rank = onehot(iota((lanes, rows), 0).astype(F32) == rank)
    stacked = jnp.concatenate([chosen * high, chosen * low, chosen], axis=0).astype(BF16)
    found = dot_t(stacked, by_rank)
    slots = found[:spaces] * 32.0 + found[spaces : 2 * spaces]
    slots = jnp.where(found[2 * spaces :] > 0.5, slots, -1.0)
    table[...] = jnp.broadcast_to(slots[:, None, :], table.shape)
    row_at = ahead.astype(F32) * float(cap) + rank

    pl.semaphore_wait(barrier, spaces - 1)

    halos = []
    for b in range(bricks):
        for source, dst, step, n in (
            (b * brick + brick - face, halo_l, 1, 2 * b),
            (b * brick, halo_r, spaces - 1, 2 * b + 1),
        ):
            copy = pltpu.make_async_remote_copy(
                src_ref=feat.at[pl.ds(source, face)], dst_ref=dst.at[b], send_sem=hs.at[n], recv_sem=hr.at[n],
                device_id=peer(step), device_id_type=MESH,
            )
            copy.start()
            halos.append(copy)

    def table_copy(k):
        return pltpu.make_async_remote_copy(
            src_ref=table.at[k], dst_ref=got.at[k], send_sem=ts.at[k], recv_sem=tr.at[k],
            device_id=peer(k), device_id_type=MESH,
        )

    def row_copy(k):
        return pltpu.make_async_remote_copy(
            src_ref=send.at[k], dst_ref=recv.at[k], send_sem=rs.at[k], recv_sem=rr.at[k],
            device_id=peer(k), device_id_type=MESH,
        )

    def start_table(k, carry):
        table_copy(k).start()
        return carry

    lax.fori_loop(1, spaces, start_table, 0)

    depth = iota((EDGE + 2, EDGE, width), 1)

    def beside(b, offset, source_id):
        p, q, r = offset
        number = 9 * (p + 1) + 3 * (q + 1) + (r + 1)
        number -= number > 13
        target = nb[b, number]
        return jnp.where((target == source_id) & (target >= 0), 1.0, 0.0)

    def layer(ref, first):
        return ref[pl.ds(first, face)].astype(F32).reshape(EDGE, EDGE, width)

    def write_layer(b, i, p, sources, ids, own):
        grown = []
        for r in (-1, 0, 1):
            parts = []
            for q in (-1, 0, 1):
                part = slice(EDGE - 1, EDGE) if q < 0 else slice(0, 1) if q > 0 else slice(0, EDGE)
                if own is not None and q == 0 and r == 0:
                    parts.append(own)
                    continue
                total = None
                for source, one_id in zip(sources, ids):
                    term = source[part] * beside(b, (p, q, r), one_id)
                    total = term if total is None else total + term
                parts.append(total)
            grown.append(jnp.concatenate(parts, axis=0))
        below, here, above = grown
        variants = (
            pltpu.roll(jnp.where(depth == EDGE - 1, below, here), 1, 1),
            here,
            pltpu.roll(jnp.where(depth == 0, above, here), EDGE - 1, 1),
        )
        first = i * face if isinstance(i, int) else pl.multiple_of(i * face, face)
        for q in range(3):
            for r in range(3):
                n = 3 * q + r
                x[b, pl.ds(first, face), n * width : (n + 1) * width] = (
                    variants[r][q : q + EDGE].reshape(face, width).astype(BF16)
                )

    own_ids = [me * bricks + n for n in range(bricks)]
    left_ids = [(me - 1) * bricks + n for n in range(bricks)]
    right_ids = [(me + 1) * bricks + n for n in range(bricks)]

    def inner(i, carry):
        sources = [layer(feat, pl.multiple_of(n * brick + i * face, face)) for n in range(bricks)]
        for b in range(bricks):
            write_layer(b, i + 1, 0, sources, own_ids, sources[b])
        return carry

    lax.fori_loop(0, EDGE, inner, 0)

    for copy in halos:
        copy.wait_recv()
    tops = [layer(feat, n * brick + brick - face) for n in range(bricks)]
    bottoms = [layer(feat, n * brick) for n in range(bricks)]
    lefts = [layer(halo_l.at[n], 0) for n in range(bricks)]
    rights = [layer(halo_r.at[n], 0) for n in range(bricks)]
    for b in range(bricks):
        write_layer(b, 0, -1, lefts + tops, left_ids + own_ids, None)
        write_layer(b, EDGE + 1, 1, bottoms + rights, own_ids + right_ids, None)

    load.wait()
    tile = 256

    def conv(n, carry):
        b, first = n // (brick // tile), n % (brick // tile) * tile
        acc = jnp.zeros((tile, width), F32)
        for p in range(3):
            window = x[b, pl.ds(pl.multiple_of(first + p * face, face), tile), :]
            acc = acc + dot(window, w[9 * p : 9 * p + 9].reshape(9 * width, width))
        at = pl.ds(pl.multiple_of(n * tile, tile), tile)
        enc[at] = (feat[at].astype(F32) + acc).astype(BF16)
        return carry

    lax.fori_loop(0, rows // tile, conv, 0)

    group = 8
    for c in range(spaces // group):
        wanted = (iota((group * cap, rows), 0) + c * group * cap).astype(F32)
        block = dot(onehot(wanted == row_at), enc[...]).astype(BF16)
        send[c * group : (c + 1) * group] = block.reshape(group, cap, width)
        for k in range(max(1, c * group), (c + 1) * group):
            row_copy(k).start()
    recv[0] = send[0]
    got[0] = table[0]

    def wait_table(k, carry):
        table_copy(k).wait()
        return carry

    lax.fori_loop(1, spaces, wait_table, 0)
    total = jnp.zeros((rows, width), F32)
    column = iota((8, 128), 1)
    for c in range(spaces // group):
        for k in range(max(1, c * group), (c + 1) * group):
            row_copy(k).wait_recv()
        blocks = []
        for t in range(c * group * cap // 128, (c + 1) * group * cap // 128):
            lane = jnp.full((8, 128), -1.0, F32)
            for k in range(spaces):
                start, end = max(0, k * cap - 128 * t), min(128, (k + 1) * cap - 128 * t)
                if start >= end:
                    continue
                moved = got[k]
                if (k * cap - 128 * t) % 128:
                    moved = pltpu.roll(moved, (k * cap - 128 * t) % 128, 1)
                lane = jnp.where((column >= start) & (column < end), moved, lane)
            blocks.append(onehot(iota((rows, 128), 0).astype(F32) == lane[0:1]))
        arrived = recv[c * group : (c + 1) * group].reshape(group * cap, width)
        total = total + dot(jnp.concatenate(blocks, axis=1), arrived)
    reg[...] = total.astype(BF16)

    def wait_sent(k, carry):
        row_copy(k).wait_send()
        return carry

    lax.fori_loop(1, spaces, wait_sent, 0)
    for copy in halos:
        copy.wait_send()


def front(features, neighbours, order, weight):
    spaces = lax.axis_size("space")
    rows, width = features.shape
    cap = 3 * rows // (2 * spaces)
    bricks = rows // EDGE**3
    face = EDGE * EDGE
    vmem = pl.BlockSpec(memory_space=pltpu.VMEM)
    return pl.pallas_call(
        functools.partial(front_kernel, spaces, cap),
        out_shape=[jax.ShapeDtypeStruct((rows, width), BF16)] * 2,
        in_specs=[vmem, pl.BlockSpec(memory_space=pltpu.SMEM), vmem, pl.BlockSpec(memory_space=pl.ANY)],
        out_specs=[vmem, vmem],
        scratch_shapes=[
            pltpu.VMEM(weight.shape, BF16),
            pltpu.VMEM((bricks, (EDGE + 2) * face, 9 * width), BF16),
            pltpu.VMEM((bricks, face, width), BF16),
            pltpu.VMEM((bricks, face, width), BF16),
            pltpu.VMEM((spaces, 8, 128), F32),
            pltpu.VMEM((spaces, 8, 128), F32),
            pltpu.VMEM((spaces, cap, width), BF16),
            pltpu.VMEM((spaces, cap, width), BF16),
            pltpu.SemaphoreType.DMA,
            pltpu.SemaphoreType.DMA((2 * bricks,)),
            pltpu.SemaphoreType.DMA((2 * bricks,)),
            pltpu.SemaphoreType.DMA((spaces,)),
            pltpu.SemaphoreType.DMA((spaces,)),
            pltpu.SemaphoreType.DMA((spaces,)),
            pltpu.SemaphoreType.DMA((spaces,)),
        ],
        compiler_params=pltpu.CompilerParams(collective_id=0, has_side_effects=True, vmem_limit_bytes=VMEM_LIMIT),
        cost_estimate=pl.CostEstimate(
            flops=2 * rows * 27 * width * width, bytes_accessed=weight.size * 2 + 6 * rows * width, transcendentals=0
        ),
        name="front",
    )(features, neighbours, order, weight)


def attention_kernel(
    spaces, reps, reg, wi, wo, cot, att, grad,
    q, k, v, ctx, s0, s1, term, first, part, second, final, tail, tail_one, tail_two,
    sa, ra, sb, rb, sc, rc, sd, rd, se, re,
):
    rows, width = reg.shape
    head = width // HEADS
    half = width // 2
    space, rep = lax.axis_index("space"), lax.axis_index("rep")
    planes, others = spaces // 2, 2 * reps
    chip, core = space // 2, space % 2
    place = rep * 2 + core

    def across(n):
        return {"space": lax.rem(chip + n, planes) * 2 + core}

    def along(n):
        there = lax.rem(place + n, others)
        return {"space": chip * 2 + there % 2, "rep": there // 2}

    def run(count, make):
        def body(n, carry):
            make(n)
            return carry

        lax.fori_loop(1, count, body, 0)

    barrier = pltpu.get_barrier_semaphore()
    run(planes, lambda n: pl.semaphore_signal(barrier, inc=1, device_id=across(n), device_id_type=MESH))
    run(others, lambda n: pl.semaphore_signal(barrier, inc=1, device_id=along(n), device_id_type=MESH))

    def copy(src, dst, send, recv, device):
        return pltpu.make_async_remote_copy(
            src_ref=src, dst_ref=dst, send_sem=send, recv_sem=recv, device_id=device, device_id_type=MESH
        )

    def scatter(c, n):
        return copy(term.at[c, lax.rem(chip + n, planes)], first.at[c, n], sa.at[c, n], ra.at[c, n], across(n))

    def share(c, n):
        return copy(part.at[c], second.at[c, place], sb.at[c, n], rb.at[c, n], along(n))

    def shared(c, n):
        there = lax.rem(place - n + others, others)
        return copy(part.at[c], second.at[c, there], sb.at[c, n], rb.at[c, n], along(n))

    def gather(c, n):
        return copy(final.at[c, chip], final.at[c, chip], sc.at[c, n], rc.at[c, n], across(n))

    def gathered(c, n):
        there = lax.rem(chip - n + planes, planes)
        return copy(final.at[c, there], final.at[c, there], sc.at[c, n], rc.at[c, n], across(n))

    def share_tail(n):
        return copy(tail.at[0], tail_one.at[place], sd.at[n], rd.at[n], along(n))

    def shared_tail(n):
        there = lax.rem(place - n + others, others)
        return copy(tail.at[0], tail_one.at[there], sd.at[n], rd.at[n], along(n))

    def gather_tail(n):
        return copy(tail.at[1], tail_two.at[chip], se.at[n], re.at[n], across(n))

    def gathered_tail(n):
        there = lax.rem(chip - n + planes, planes)
        return copy(tail.at[1], tail_two.at[there], se.at[n], re.at[n], across(n))

    def finish_scatter(c):
        first[c, 0] = term[c, chip]
        run(planes, lambda n: scatter(c, n).wait())
        part[c] = jnp.sum(first[c], axis=0)
        run(others, lambda n: share(c, n).start())

    def finish_share(c):
        second[c, place] = part[c]
        run(others, lambda n: share(c, n).wait_send())
        run(others, lambda n: shared(c, n).wait_recv())
        final[c, chip] = jnp.sum(second[c], axis=0)
        run(planes, lambda n: gather(c, n).start())

    def finish_gather(c):
        run(planes, lambda n: gather(c, n).wait_send())
        run(planes, lambda n: gathered(c, n).wait_recv())

    def gradient_rows(side):
        part_context = ctx[side].astype(BF16)
        return lax.dot_general(part_context, cot[...], (((0,), (0,)), ((), ())), preferred_element_type=F32)

    residual = reg[...].astype(F32)
    centred = residual - jnp.mean(residual, axis=-1, keepdims=True)
    variance = jnp.mean(centred * centred, axis=-1, keepdims=True)
    normed = (centred * lax.rsqrt(variance + 1e-05)).astype(BF16)
    packed = dot(normed, wi[...]).astype(BF16)
    q[...] = packed[:, :width] * jnp.asarray(head**-0.5, BF16)
    k[...] = packed[:, width : 2 * width]
    ones = jnp.ones((rows, half), BF16)
    for n in range(2):
        v[n] = jnp.concatenate([packed[:, 2 * width + n * half : 2 * width + (n + 1) * half], ones], axis=1)
    ctx[...] = jnp.zeros_like(ctx)
    tile = s0.shape[0]
    tiles = rows // tile
    lane_q = iota((tile, width), 1) // head
    lane_c = iota((tile, half), 1) // head
    held = (s0, s1)

    def scores(h, t):
        queries = jnp.where(lane_q == h, q[t * tile : (t + 1) * tile], jnp.zeros((), BF16))
        return dot_t(queries, k[...])

    def one_head(h):
        side = h // (HEADS // 2)
        for t in range(tiles):
            later = h if t < tiles - 1 else jnp.minimum(h + 1, HEADS - 1)
            held[(t + 1) % 2][...] = scores(later, (t + 1) % tiles)
            now = held[t % 2][...]
            lifted = jnp.exp(now - jnp.max(now, axis=-1, keepdims=True))
            both = dot(lifted.astype(BF16), v[side])
            at = slice(t * tile, (t + 1) * tile)
            ctx[side, at] += jnp.where(lane_c == h - side * (HEADS // 2), both[:, :half] / both[:, half:], 0.0)

    s0[...] = scores(0, 0)
    blocks = term.shape[2]
    steps = HEADS // 2

    def step(n, carry):
        one_head(2 * n)
        one_head(2 * n + 1)

        @pl.when(n == steps // 2 - 1)
        def _():
            term[0] = gradient_rows(0).reshape(planes, blocks, width)
            pl.semaphore_wait(barrier, planes + others - 2)
            run(planes, lambda m: scatter(0, m).start())

        @pl.when(n == steps // 2)
        def _():
            finish_scatter(0)

        @pl.when(n == steps // 2 + 1)
        def _():
            finish_share(0)

        @pl.when(n == steps - 2)
        def _():
            term[1] = gradient_rows(1).reshape(planes, blocks, width)
            run(planes, lambda m: scatter(1, m).start())

        return carry

    lax.fori_loop(0, steps, step, 0)
    left = tail.shape[1]
    tail[0] = gradient_rows(1)[half - left :]
    run(others, lambda n: share_tail(n).start())
    finish_scatter(1)
    context = jnp.concatenate([ctx[0], ctx[1]], axis=1).astype(BF16)
    att[...] = (reg[...].astype(F32) + dot(context, wo[...])).astype(BF16)
    tail_one[place] = tail[0]
    run(others, lambda n: share_tail(n).wait_send())
    run(others, lambda n: shared_tail(n).wait_recv())
    tail[1] = jnp.sum(tail_one[...], axis=0)
    run(planes, lambda n: gather_tail(n).start())
    finish_share(1)
    finish_gather(0)
    grad[:half] = final[0].reshape(half, width)
    finish_gather(1)
    grad[half : width - left] = final[1].reshape(half, width)[: half - left]
    tail_two[chip] = tail[1]
    run(planes, lambda n: gather_tail(n).wait_send())
    run(planes, lambda n: gathered_tail(n).wait_recv())
    grad[width - left :] = jnp.sum(tail_two[...], axis=0)


def attention(regrouped, wi, wo, cot):
    spaces, reps = lax.axis_size("space"), lax.axis_size("rep")
    rows, width = regrouped.shape
    head, half = width // HEADS, width // 2
    planes, others = spaces // 2, 2 * reps
    block, left, tile = half // planes, 2 * head, 256
    vmem = pl.BlockSpec(memory_space=pltpu.VMEM)
    dma = pltpu.SemaphoreType.DMA
    return pl.pallas_call(
        functools.partial(attention_kernel, spaces, reps),
        out_shape=[jax.ShapeDtypeStruct((rows, width), BF16), jax.ShapeDtypeStruct((width, width), F32)],
        in_specs=[vmem] * 4,
        out_specs=[vmem, vmem],
        scratch_shapes=[
            pltpu.VMEM((rows, width), BF16),
            pltpu.VMEM((rows, width), BF16),
            pltpu.VMEM((2, rows, width), BF16),
            pltpu.VMEM((2, rows, half), F32),
            pltpu.VMEM((tile, rows), F32),
            pltpu.VMEM((tile, rows), F32),
            pltpu.VMEM((2, planes, block, width), F32),
            pltpu.VMEM((2, planes, block, width), F32),
            pltpu.VMEM((2, block, width), F32),
            pltpu.VMEM((2, others, block, width), F32),
            pltpu.VMEM((2, planes, block, width), F32),
            pltpu.VMEM((2, left, width), F32),
            pltpu.VMEM((others, left, width), F32),
            pltpu.VMEM((planes, left, width), F32),
        ]
        + [dma((2, planes))] * 2
        + [dma((2, others))] * 2
        + [dma((2, planes))] * 2
        + [dma((others,))] * 2
        + [dma((planes,))] * 2,
        compiler_params=pltpu.CompilerParams(collective_id=1, has_side_effects=True, vmem_limit_bytes=VMEM_LIMIT),
        cost_estimate=pl.CostEstimate(
            flops=4 * HEADS * rows * rows * width, bytes_accessed=8 * rows * width, transcendentals=HEADS * rows * rows
        ),
        name="attention",
    )(regrouped, wi, wo, cot)


def local(features, neighbours, serial_order, kernel_weight, input_projection, output_projection, cotangent):
    encoded, regrouped = front(features[0], neighbours[0], serial_order, kernel_weight)
    attended, gradient = attention(regrouped, input_projection, output_projection, cotangent[0])
    return encoded[None], attended[None], gradient


def solution(mesh):
    in_specs = (
        P("rep", "space", None),
        P("rep", "space", None),
        P("rep", "space"),
        P(),
        P(),
        P(),
        P("rep", "space", None),
    )
    out_specs = (P("rep", "space", None), P("rep", "space", None), P())
    return jax.shard_map(local, mesh=mesh, in_specs=in_specs, out_specs=out_specs, check_vma=False)
```

```python
import functools

import jax
import jax.numpy as jnp
from jax import lax
from jax.experimental import pallas as pl
from jax.experimental.pallas import tpu as pltpu
from jax.sharding import PartitionSpec as P

HEADS = 16
EDGE = 8
MESH = pl.DeviceIdType.MESH
F32 = jnp.float32
BF16 = jnp.bfloat16
VMEM_LIMIT = 60 * 1024 * 1024


def dot(a, b):
    return jnp.dot(a, b, preferred_element_type=F32)


def dot_t(a, b):
    return lax.dot_general(a, b, (((1,), (1,)), ((), ())), preferred_element_type=F32)


def iota(shape, dim):
    return lax.broadcasted_iota(jnp.int32, shape, dim)


def onehot(mask):
    return jnp.where(mask, 1.0, 0.0).astype(BF16)


def front_kernel(
    spaces, cap, feat, nb, order, w_hbm, enc, reg,
    w, x, halo_l, halo_r, table, got, send, recv, place,
    w_sem, hs, hr, ts, tr, rs, rr,
):
    me = lax.axis_index("space")
    rows, width = feat.shape
    face = EDGE * EDGE
    brick = EDGE * face
    bricks = rows // brick
    load = pltpu.make_async_copy(w_hbm, w, w_sem)
    load.start()

    def peer(k):
        return {"space": lax.rem(me + k, spaces)}

    barrier = pltpu.get_barrier_semaphore()

    def greet(k, carry):
        pl.semaphore_signal(barrier, inc=1, device_id=peer(k), device_id_type=MESH)
        return carry

    lax.fori_loop(1, spaces, greet, 0)

    depth = iota((EDGE + 2, EDGE, width), 1)

    def beside(b, offset, source_id):
        p, q, r = offset
        number = 9 * (p + 1) + 3 * (q + 1) + (r + 1)
        number -= number > 13
        target = nb[b, number]
        return jnp.where((target == source_id) & (target >= 0), 1.0, 0.0)

    def layer(ref, first):
        return ref[pl.ds(first, face)].astype(F32).reshape(EDGE, EDGE, width)

    def write_layer(b, i, p, sources, ids, own):
        grown = []
        for r in (-1, 0, 1):
            parts = []
            for q in (-1, 0, 1):
                part = slice(EDGE - 1, EDGE) if q < 0 else slice(0, 1) if q > 0 else slice(0, EDGE)
                if own is not None and q == 0 and r == 0:
                    parts.append(own)
                    continue
                total = None
                for source, one_id in zip(sources, ids):
                    term = source[part] * beside(b, (p, q, r), one_id)
                    total = term if total is None else total + term
                parts.append(total)
            grown.append(jnp.concatenate(parts, axis=0))
        below, here, above = grown
        variants = (
            pltpu.roll(jnp.where(depth == EDGE - 1, below, here), 1, 1),
            here,
            pltpu.roll(jnp.where(depth == 0, above, here), EDGE - 1, 1),
        )
        first = i * face if isinstance(i, int) else pl.multiple_of(i * face, face)
        for q in range(3):
            for r in range(3):
                n = 3 * q + r
                x[b, pl.ds(first, face), n * width : (n + 1) * width] = (
                    variants[r][q : q + EDGE].reshape(face, width).astype(BF16)
                )

    own_ids = [me * bricks + n for n in range(bricks)]
    left_ids = [(me - 1) * bricks + n for n in range(bricks)]
    right_ids = [(me + 1) * bricks + n for n in range(bricks)]

    def inner(i, carry):
        sources = [layer(feat, pl.multiple_of(n * brick + i * face, face)) for n in range(bricks)]
        for b in range(bricks):
            write_layer(b, i + 1, 0, sources, own_ids, sources[b])
        return carry

    lax.fori_loop(0, EDGE, inner, 0)

    places = order[...]
    shift = rows.bit_length() - 1
    owner = lax.shift_right_logical(places, shift)
    slot = places & (rows - 1)
    ahead = (owner - me + spaces) & (spaces - 1)
    chosen = jnp.where(iota((spaces, rows), 0) == ahead, 1.0, 0.0)
    before = onehot(iota((rows, rows), 0) < iota((rows, rows), 1))
    rank = jnp.sum(chosen * dot(chosen.astype(BF16), before), axis=0, keepdims=True)
    high = lax.shift_right_logical(slot, 5).astype(F32)
    low = (slot & 31).astype(F32)
    lanes = table.shape[2]
    by_rank = onehot(iota((lanes, rows), 0).astype(F32) == rank)
    stacked = jnp.concatenate([chosen * high, chosen * low, chosen], axis=0).astype(BF16)
    found = dot_t(stacked, by_rank)
    slots = found[:spaces] * 32.0 + found[spaces : 2 * spaces]
    slots = jnp.where(found[2 * spaces :] > 0.5, slots, -1.0)
    table[...] = jnp.broadcast_to(slots[:, None, :], table.shape)
    row_at = ahead.astype(F32) * float(cap) + rank

    pl.semaphore_wait(barrier, spaces - 1)

    halos = []
    for b in range(bricks):
        for source, dst, step, n in (
            (b * brick + brick - face, halo_l, 1, 2 * b),
            (b * brick, halo_r, spaces - 1, 2 * b + 1),
        ):
            copy = pltpu.make_async_remote_copy(
                src_ref=feat.at[pl.ds(source, face)], dst_ref=dst.at[b], send_sem=hs.at[n], recv_sem=hr.at[n],
                device_id=peer(step), device_id_type=MESH,
            )
            copy.start()
            halos.append(copy)

    def table_copy(k):
        return pltpu.make_async_remote_copy(
            src_ref=table.at[k], dst_ref=got.at[k], send_sem=ts.at[k], recv_sem=tr.at[k],
            device_id=peer(k), device_id_type=MESH,
        )

    def row_copy(k):
        return pltpu.make_async_remote_copy(
            src_ref=send.at[k], dst_ref=recv.at[k], send_sem=rs.at[k], recv_sem=rr.at[k],
            device_id=peer(k), device_id_type=MESH,
        )

    def start_table(k, carry):
        table_copy(k).start()
        return carry

    lax.fori_loop(1, spaces, start_table, 0)

    def window(first, count, p):
        return pl.ds(first + p * face if isinstance(first, int) else pl.multiple_of(first + p * face, face), count)

    def products(p, rows_in):
        return dot(rows_in, w[9 * p : 9 * p + 9].reshape(9 * width, width))

    load.wait()
    middle = brick - 2 * face

    def conv_middle(b, carry):
        acc = jnp.zeros((middle, width), F32)
        for p in range(3):
            acc = acc + products(p, x[b, window(face, middle, p), :])
        at = pl.ds(pl.multiple_of(b * brick + face, face), middle)
        enc[at] = (feat[at].astype(F32) + acc).astype(BF16)
        return carry

    lax.fori_loop(0, bricks, conv_middle, 0)
    for copy in halos:
        copy.wait_recv()
    tops = [layer(feat, n * brick + brick - face) for n in range(bricks)]
    bottoms = [layer(feat, n * brick) for n in range(bricks)]
    lefts = [layer(halo_l.at[n], 0) for n in range(bricks)]
    rights = [layer(halo_r.at[n], 0) for n in range(bricks)]
    for b in range(bricks):
        write_layer(b, 0, -1, lefts + tops, left_ids + own_ids, None)
        write_layer(b, EDGE + 1, 1, bottoms + rights, own_ids + right_ids, None)

    ends = [(b, first) for b in range(bricks) for first in (0, brick - face)]
    acc = jnp.zeros((len(ends) * face, width), F32)
    for p in range(3):
        acc = acc + products(p, jnp.concatenate([x[b, window(first, face, p), :] for b, first in ends], axis=0))
    for n, (b, first) in enumerate(ends):
        at = pl.ds(b * brick + first, face)
        enc[at] = (feat[at].astype(F32) + acc[n * face : (n + 1) * face]).astype(BF16)

    group = 8
    for c in range(spaces // group):
        wanted = (iota((group * cap, rows), 0) + c * group * cap).astype(F32)
        block = dot(onehot(wanted == row_at), enc[...]).astype(BF16)
        send[c * group : (c + 1) * group] = block.reshape(group, cap, width)
        for k in range(max(1, c * group), (c + 1) * group):
            row_copy(k).start()
    recv[0] = send[0]
    got[0] = table[0]

    def wait_table(k, carry):
        table_copy(k).wait()
        return carry

    lax.fori_loop(1, spaces, wait_table, 0)
    column = iota((8, 128), 1)
    for t in range(spaces * cap // 128):
        lane = jnp.full((8, 128), -1.0, F32)
        for k in range(spaces):
            start, end = max(0, k * cap - 128 * t), min(128, (k + 1) * cap - 128 * t)
            if start >= end:
                continue
            moved = got[k]
            if (k * cap - 128 * t) % 128:
                moved = pltpu.roll(moved, (k * cap - 128 * t) % 128, 1)
            lane = jnp.where((column >= start) & (column < end), moved, lane)
        place[:, t * 128 : (t + 1) * 128] = onehot(iota((rows, 128), 0).astype(F32) == lane[0:1])
    total = jnp.zeros((rows, width), F32)
    for c in range(spaces // group):
        for k in range(max(1, c * group), (c + 1) * group):
            row_copy(k).wait_recv()
        arrived = recv[c * group : (c + 1) * group].reshape(group * cap, width)
        total = total + dot(place[:, c * group * cap : (c + 1) * group * cap], arrived)
    reg[...] = total.astype(BF16)

    def wait_sent(k, carry):
        row_copy(k).wait_send()
        return carry

    lax.fori_loop(1, spaces, wait_sent, 0)
    for copy in halos:
        copy.wait_send()


def front(features, neighbours, order, weight):
    spaces = lax.axis_size("space")
    rows, width = features.shape
    cap = 3 * rows // (2 * spaces)
    bricks = rows // EDGE**3
    face = EDGE * EDGE
    vmem = pl.BlockSpec(memory_space=pltpu.VMEM)
    return pl.pallas_call(
        functools.partial(front_kernel, spaces, cap),
        out_shape=[jax.ShapeDtypeStruct((rows, width), BF16)] * 2,
        in_specs=[vmem, pl.BlockSpec(memory_space=pltpu.SMEM), vmem, pl.BlockSpec(memory_space=pl.ANY)],
        out_specs=[vmem, vmem],
        scratch_shapes=[
            pltpu.VMEM(weight.shape, BF16),
            pltpu.VMEM((bricks, (EDGE + 2) * face, 9 * width), BF16),
            pltpu.VMEM((bricks, face, width), BF16),
            pltpu.VMEM((bricks, face, width), BF16),
            pltpu.VMEM((spaces, 8, 128), F32),
            pltpu.VMEM((spaces, 8, 128), F32),
            pltpu.VMEM((spaces, cap, width), BF16),
            pltpu.VMEM((spaces, cap, width), BF16),
            pltpu.VMEM((rows, spaces * cap), BF16),
            pltpu.SemaphoreType.DMA,
            pltpu.SemaphoreType.DMA((2 * bricks,)),
            pltpu.SemaphoreType.DMA((2 * bricks,)),
            pltpu.SemaphoreType.DMA((spaces,)),
            pltpu.SemaphoreType.DMA((spaces,)),
            pltpu.SemaphoreType.DMA((spaces,)),
            pltpu.SemaphoreType.DMA((spaces,)),
        ],
        compiler_params=pltpu.CompilerParams(collective_id=0, has_side_effects=True, vmem_limit_bytes=VMEM_LIMIT),
        cost_estimate=pl.CostEstimate(
            flops=2 * rows * 27 * width * width, bytes_accessed=weight.size * 2 + 6 * rows * width, transcendentals=0
        ),
        name="front",
    )(features, neighbours, order, weight)


def attention_kernel(
    spaces, reps, reg, wi, wo, cot, att, grad,
    q, k, v, ctx, s0, s1, term, first, part, second, final, tail, tail_one, tail_two,
    sa, ra, sb, rb, sc, rc, sd, rd, se, re,
):
    rows, width = reg.shape
    head = width // HEADS
    half = width // 2
    space, rep = lax.axis_index("space"), lax.axis_index("rep")
    planes, others = spaces // 2, 2 * reps
    chip, core = space // 2, space % 2
    place = rep * 2 + core

    def across(n):
        return {"space": lax.rem(chip + n, planes) * 2 + core}

    def along(n):
        there = lax.rem(place + n, others)
        return {"space": chip * 2 + there % 2, "rep": there // 2}

    def run(count, make):
        def body(n, carry):
            make(n)
            return carry

        lax.fori_loop(1, count, body, 0)

    barrier = pltpu.get_barrier_semaphore()
    run(planes, lambda n: pl.semaphore_signal(barrier, inc=1, device_id=across(n), device_id_type=MESH))
    run(others, lambda n: pl.semaphore_signal(barrier, inc=1, device_id=along(n), device_id_type=MESH))

    def copy(src, dst, send, recv, device):
        return pltpu.make_async_remote_copy(
            src_ref=src, dst_ref=dst, send_sem=send, recv_sem=recv, device_id=device, device_id_type=MESH
        )

    def scatter(c, n):
        return copy(term.at[c, lax.rem(chip + n, planes)], first.at[c, n], sa.at[c, n], ra.at[c, n], across(n))

    def share(c, n):
        return copy(part.at[c], second.at[c, place], sb.at[c, n], rb.at[c, n], along(n))

    def shared(c, n):
        there = lax.rem(place - n + others, others)
        return copy(part.at[c], second.at[c, there], sb.at[c, n], rb.at[c, n], along(n))

    def gather(c, n):
        return copy(final.at[c, chip], final.at[c, chip], sc.at[c, n], rc.at[c, n], across(n))

    def gathered(c, n):
        there = lax.rem(chip - n + planes, planes)
        return copy(final.at[c, there], final.at[c, there], sc.at[c, n], rc.at[c, n], across(n))

    def share_tail(n):
        return copy(tail.at[0], tail_one.at[place], sd.at[n], rd.at[n], along(n))

    def shared_tail(n):
        there = lax.rem(place - n + others, others)
        return copy(tail.at[0], tail_one.at[there], sd.at[n], rd.at[n], along(n))

    def gather_tail(n):
        return copy(tail.at[1], tail_two.at[chip], se.at[n], re.at[n], across(n))

    def gathered_tail(n):
        there = lax.rem(chip - n + planes, planes)
        return copy(tail.at[1], tail_two.at[there], se.at[n], re.at[n], across(n))

    def finish_scatter(c):
        first[c, 0] = term[c, chip]
        run(planes, lambda n: scatter(c, n).wait())
        part[c] = jnp.sum(first[c], axis=0)
        run(others, lambda n: share(c, n).start())

    def finish_share(c):
        second[c, place] = part[c]
        run(others, lambda n: share(c, n).wait_send())
        run(others, lambda n: shared(c, n).wait_recv())
        final[c, chip] = jnp.sum(second[c], axis=0)
        run(planes, lambda n: gather(c, n).start())

    def finish_gather(c):
        run(planes, lambda n: gather(c, n).wait_send())
        run(planes, lambda n: gathered(c, n).wait_recv())

    def gradient_rows(side):
        part_context = ctx[side].astype(BF16)
        return lax.dot_general(part_context, cot[...], (((0,), (0,)), ((), ())), preferred_element_type=F32)

    residual = reg[...].astype(F32)
    centred = residual - jnp.mean(residual, axis=-1, keepdims=True)
    variance = jnp.mean(centred * centred, axis=-1, keepdims=True)
    normed = (centred * lax.rsqrt(variance + 1e-05)).astype(BF16)
    packed = dot(normed, wi[...]).astype(BF16)
    q[...] = packed[:, :width] * jnp.asarray(head**-0.5, BF16)
    k[...] = packed[:, width : 2 * width]
    ones = jnp.ones((rows, half), BF16)
    for n in range(2):
        v[n] = jnp.concatenate([packed[:, 2 * width + n * half : 2 * width + (n + 1) * half], ones], axis=1)
    ctx[...] = jnp.zeros_like(ctx)
    tile = s0.shape[0]
    tiles = rows // tile
    lane_q = iota((tile, width), 1) // head
    lane_c = iota((tile, half), 1) // head
    held = (s0, s1)

    def scores(h, t):
        queries = jnp.where(lane_q == h, q[t * tile : (t + 1) * tile], jnp.zeros((), BF16))
        return dot_t(queries, k[...])

    def one_head(h):
        side = h // (HEADS // 2)
        for t in range(tiles):
            later = h if t < tiles - 1 else jnp.minimum(h + 1, HEADS - 1)
            held[(t + 1) % 2][...] = scores(later, (t + 1) % tiles)
            now = held[t % 2][...]
            lifted = jnp.exp(now - jnp.max(now, axis=-1, keepdims=True))
            both = dot(lifted.astype(BF16), v[side])
            at = slice(t * tile, (t + 1) * tile)
            ctx[side, at] += jnp.where(lane_c == h - side * (HEADS // 2), both[:, :half] / both[:, half:], 0.0)

    s0[...] = scores(0, 0)
    blocks = term.shape[2]
    steps = HEADS // 2

    def step(n, carry):
        one_head(2 * n)
        one_head(2 * n + 1)

        @pl.when(n == steps // 2 - 1)
        def _():
            term[0] = gradient_rows(0).reshape(planes, blocks, width)
            pl.semaphore_wait(barrier, planes + others - 2)
            run(planes, lambda m: scatter(0, m).start())

        @pl.when(n == steps // 2 + 1)
        def _():
            finish_scatter(0)

        @pl.when(n == steps - 2)
        def _():
            term[1] = gradient_rows(1).reshape(planes, blocks, width)
            run(planes, lambda m: scatter(1, m).start())

        return carry

    lax.fori_loop(0, steps, step, 0)
    left = tail.shape[1]
    tail[0] = gradient_rows(1)[half - left :].astype(BF16)
    run(others, lambda n: share_tail(n).start())
    finish_share(0)
    context = jnp.concatenate([ctx[0], ctx[1]], axis=1).astype(BF16)
    att[...] = (reg[...].astype(F32) + dot(context, wo[...])).astype(BF16)
    finish_scatter(1)
    tail_one[place] = tail[0]
    run(others, lambda n: share_tail(n).wait_send())
    run(others, lambda n: shared_tail(n).wait_recv())
    tail[1] = jnp.sum(tail_one[...].astype(F32), axis=0).astype(BF16)
    run(planes, lambda n: gather_tail(n).start())
    finish_share(1)
    finish_gather(0)
    grad[:half] = final[0].reshape(half, width)
    finish_gather(1)
    grad[half : width - left] = final[1].reshape(half, width)[: half - left]
    tail_two[chip] = tail[1]
    run(planes, lambda n: gather_tail(n).wait_send())
    run(planes, lambda n: gathered_tail(n).wait_recv())
    grad[width - left :] = jnp.sum(tail_two[...].astype(F32), axis=0)


def attention(regrouped, wi, wo, cot):
    spaces, reps = lax.axis_size("space"), lax.axis_size("rep")
    rows, width = regrouped.shape
    head, half = width // HEADS, width // 2
    planes, others = spaces // 2, 2 * reps
    block, left, tile = half // planes, 2 * head, 256
    vmem = pl.BlockSpec(memory_space=pltpu.VMEM)
    dma = pltpu.SemaphoreType.DMA
    return pl.pallas_call(
        functools.partial(attention_kernel, spaces, reps),
        out_shape=[jax.ShapeDtypeStruct((rows, width), BF16), jax.ShapeDtypeStruct((width, width), F32)],
        in_specs=[vmem] * 4,
        out_specs=[vmem, vmem],
        scratch_shapes=[
            pltpu.VMEM((rows, width), BF16),
            pltpu.VMEM((rows, width), BF16),
            pltpu.VMEM((2, rows, width), BF16),
            pltpu.VMEM((2, rows, half), F32),
            pltpu.VMEM((tile, rows), F32),
            pltpu.VMEM((tile, rows), F32),
            pltpu.VMEM((2, planes, block, width), F32),
            pltpu.VMEM((2, planes, block, width), F32),
            pltpu.VMEM((2, block, width), F32),
            pltpu.VMEM((2, others, block, width), F32),
            pltpu.VMEM((2, planes, block, width), F32),
            pltpu.VMEM((2, left, width), BF16),
            pltpu.VMEM((others, left, width), BF16),
            pltpu.VMEM((planes, left, width), BF16),
        ]
        + [dma((2, planes))] * 2
        + [dma((2, others))] * 2
        + [dma((2, planes))] * 2
        + [dma((others,))] * 2
        + [dma((planes,))] * 2,
        compiler_params=pltpu.CompilerParams(collective_id=1, has_side_effects=True, vmem_limit_bytes=VMEM_LIMIT),
        cost_estimate=pl.CostEstimate(
            flops=4 * HEADS * rows * rows * width, bytes_accessed=8 * rows * width, transcendentals=HEADS * rows * rows
        ),
        name="attention",
    )(regrouped, wi, wo, cot)


def publish_kernel(count, *refs):
    copies = [pltpu.make_async_copy(refs[n], refs[count + n], refs[2 * count].at[n]) for n in range(count)]
    for copy in copies:
        copy.start()
    for copy in copies:
        copy.wait()


def publish(*arrays):
    spec = pl.BlockSpec(memory_space=pl.ANY)
    return pl.pallas_call(
        functools.partial(publish_kernel, len(arrays)),
        out_shape=[jax.ShapeDtypeStruct(a.shape, a.dtype) for a in arrays],
        in_specs=[spec] * len(arrays),
        out_specs=[spec] * len(arrays),
        scratch_shapes=[pltpu.SemaphoreType.DMA((len(arrays),))],
        name="publish",
    )(*arrays)


def local(features, neighbours, serial_order, kernel_weight, input_projection, output_projection, cotangent):
    encoded, regrouped = front(features[0], neighbours[0], serial_order, kernel_weight)
    attended, gradient = attention(regrouped, input_projection, output_projection, cotangent[0])
    encoded, attended, gradient = publish(encoded, attended, gradient)
    return encoded[None], attended[None], gradient


def solution(mesh):
    in_specs = (
        P("rep", "space", None),
        P("rep", "space", None),
        P("rep", "space"),
        P(),
        P(),
        P(),
        P("rep", "space", None),
    )
    out_specs = (P("rep", "space", None), P("rep", "space", None), P())
    return jax.shard_map(local, mesh=mesh, in_specs=in_specs, out_specs=out_specs, check_vma=False)
```

```python
import functools

import jax
import jax.numpy as jnp
from jax import lax
from jax.experimental import pallas as pl
from jax.experimental.pallas import tpu as pltpu
from jax.sharding import PartitionSpec as P

HEADS = 16
EDGE = 8
MESH = pl.DeviceIdType.MESH
F32 = jnp.float32
BF16 = jnp.bfloat16
VMEM_LIMIT = 60 * 1024 * 1024


def dot(a, b):
    return jnp.dot(a, b, preferred_element_type=F32)


def dot_t(a, b):
    return lax.dot_general(a, b, (((1,), (1,)), ((), ())), preferred_element_type=F32)


def iota(shape, dim):
    return lax.broadcasted_iota(jnp.int32, shape, dim)


def onehot(mask):
    return jnp.where(mask, 1.0, 0.0).astype(BF16)


def front_kernel(
    spaces, cap, feat, nb, order, w_hbm, enc, reg,
    w, x, halo_l, halo_r, table, got, send, recv, place,
    w_sem, hs, hr, ts, tr, rs, rr,
):
    me = lax.axis_index("space")
    rows, width = feat.shape
    face = EDGE * EDGE
    brick = EDGE * face
    bricks = rows // brick
    load = pltpu.make_async_copy(w_hbm, w, w_sem)
    load.start()

    def peer(k):
        return {"space": lax.rem(me + k, spaces)}

    barrier = pltpu.get_barrier_semaphore()

    def greet(k, carry):
        pl.semaphore_signal(barrier, inc=1, device_id=peer(k), device_id_type=MESH)
        return carry

    lax.fori_loop(1, spaces, greet, 0)

    depth = iota((EDGE + 2, EDGE, width), 1)

    def beside(b, offset, source_id):
        p, q, r = offset
        number = 9 * (p + 1) + 3 * (q + 1) + (r + 1)
        number -= number > 13
        target = nb[b, number]
        return jnp.where((target == source_id) & (target >= 0), 1.0, 0.0)

    def layer(ref, first):
        return ref[pl.ds(first, face)].astype(F32).reshape(EDGE, EDGE, width)

    def write_layer(b, i, p, sources, ids, own):
        grown = []
        for r in (-1, 0, 1):
            parts = []
            for q in (-1, 0, 1):
                part = slice(EDGE - 1, EDGE) if q < 0 else slice(0, 1) if q > 0 else slice(0, EDGE)
                if own is not None and q == 0 and r == 0:
                    parts.append(own)
                    continue
                total = None
                for source, one_id in zip(sources, ids):
                    term = source[part] * beside(b, (p, q, r), one_id)
                    total = term if total is None else total + term
                parts.append(total)
            grown.append(jnp.concatenate(parts, axis=0))
        below, here, above = grown
        variants = (
            pltpu.roll(jnp.where(depth == EDGE - 1, below, here), 1, 1),
            here,
            pltpu.roll(jnp.where(depth == 0, above, here), EDGE - 1, 1),
        )
        first = i * face if isinstance(i, int) else pl.multiple_of(i * face, face)
        for q in range(3):
            for r in range(3):
                n = 3 * q + r
                x[b, pl.ds(first, face), n * width : (n + 1) * width] = (
                    variants[r][q : q + EDGE].reshape(face, width).astype(BF16)
                )

    own_ids = [me * bricks + n for n in range(bricks)]
    left_ids = [(me - 1) * bricks + n for n in range(bricks)]
    right_ids = [(me + 1) * bricks + n for n in range(bricks)]

    def inner(i, carry):
        sources = [layer(feat, pl.multiple_of(n * brick + i * face, face)) for n in range(bricks)]
        for b in range(bricks):
            write_layer(b, i + 1, 0, sources, own_ids, sources[b])
        return carry

    lax.fori_loop(0, EDGE, inner, 0)

    places = order[...]
    shift = rows.bit_length() - 1
    owner = lax.shift_right_logical(places, shift)
    slot = places & (rows - 1)
    ahead = (owner - me + spaces) & (spaces - 1)
    chosen = jnp.where(iota((spaces, rows), 0) == ahead, 1.0, 0.0)
    before = onehot(iota((rows, rows), 0) < iota((rows, rows), 1))
    rank = jnp.sum(chosen * dot(chosen.astype(BF16), before), axis=0, keepdims=True)
    high = lax.shift_right_logical(slot, 5).astype(F32)
    low = (slot & 31).astype(F32)
    lanes = table.shape[2]
    by_rank = onehot(iota((lanes, rows), 0).astype(F32) == rank)
    stacked = jnp.concatenate([chosen * high, chosen * low, chosen], axis=0).astype(BF16)
    found = dot_t(stacked, by_rank)
    slots = found[:spaces] * 32.0 + found[spaces : 2 * spaces]
    slots = jnp.where(found[2 * spaces :] > 0.5, slots, -1.0)
    table[...] = jnp.broadcast_to(slots[:, None, :], table.shape)
    row_at = ahead.astype(F32) * float(cap) + rank

    pl.semaphore_wait(barrier, spaces - 1)

    halos = []
    for b in range(bricks):
        for source, dst, step, n in (
            (b * brick + brick - face, halo_l, 1, 2 * b),
            (b * brick, halo_r, spaces - 1, 2 * b + 1),
        ):
            copy = pltpu.make_async_remote_copy(
                src_ref=feat.at[pl.ds(source, face)], dst_ref=dst.at[b], send_sem=hs.at[n], recv_sem=hr.at[n],
                device_id=peer(step), device_id_type=MESH,
            )
            copy.start()
            halos.append(copy)

    def table_copy(k):
        return pltpu.make_async_remote_copy(
            src_ref=table.at[k], dst_ref=got.at[k], send_sem=ts.at[k], recv_sem=tr.at[k],
            device_id=peer(k), device_id_type=MESH,
        )

    def row_copy(k):
        return pltpu.make_async_remote_copy(
            src_ref=send.at[k], dst_ref=recv.at[k], send_sem=rs.at[k], recv_sem=rr.at[k],
            device_id=peer(k), device_id_type=MESH,
        )

    def start_table(k, carry):
        table_copy(k).start()
        return carry

    lax.fori_loop(1, spaces, start_table, 0)

    def window(first, count, p):
        return pl.ds(first + p * face if isinstance(first, int) else pl.multiple_of(first + p * face, face), count)

    def products(p, rows_in):
        return dot(rows_in, w[9 * p : 9 * p + 9].reshape(9 * width, width))

    load.wait()
    middle = brick - 2 * face

    def conv_middle(b, carry):
        acc = jnp.zeros((middle, width), F32)
        for p in range(3):
            acc = acc + products(p, x[b, window(face, middle, p), :])
        at = pl.ds(pl.multiple_of(b * brick + face, face), middle)
        enc[at] = (feat[at].astype(F32) + acc).astype(BF16)
        return carry

    lax.fori_loop(0, bricks, conv_middle, 0)
    for copy in halos:
        copy.wait_recv()
    tops = [layer(feat, n * brick + brick - face) for n in range(bricks)]
    bottoms = [layer(feat, n * brick) for n in range(bricks)]
    lefts = [layer(halo_l.at[n], 0) for n in range(bricks)]
    rights = [layer(halo_r.at[n], 0) for n in range(bricks)]
    for b in range(bricks):
        write_layer(b, 0, -1, lefts + tops, left_ids + own_ids, None)
        write_layer(b, EDGE + 1, 1, bottoms + rights, own_ids + right_ids, None)

    ends = [(b, first) for b in range(bricks) for first in (0, brick - face)]
    acc = jnp.zeros((len(ends) * face, width), F32)
    for p in range(3):
        acc = acc + products(p, jnp.concatenate([x[b, window(first, face, p), :] for b, first in ends], axis=0))
    for n, (b, first) in enumerate(ends):
        at = pl.ds(b * brick + first, face)
        enc[at] = (feat[at].astype(F32) + acc[n * face : (n + 1) * face]).astype(BF16)

    group = 8
    for c in range(spaces // group):
        wanted = (iota((group * cap, rows), 0) + c * group * cap).astype(F32)
        block = dot(onehot(wanted == row_at), enc[...]).astype(BF16)
        send[c * group : (c + 1) * group] = block.reshape(group, cap, width)
        for k in range(max(1, c * group), (c + 1) * group):
            row_copy(k).start()
    recv[0] = send[0]
    got[0] = table[0]

    def wait_table(k, carry):
        table_copy(k).wait()
        return carry

    lax.fori_loop(1, spaces, wait_table, 0)
    column = iota((8, 128), 1)
    for t in range(spaces * cap // 128):
        lane = jnp.full((8, 128), -1.0, F32)
        for k in range(spaces):
            start, end = max(0, k * cap - 128 * t), min(128, (k + 1) * cap - 128 * t)
            if start >= end:
                continue
            moved = got[k]
            if (k * cap - 128 * t) % 128:
                moved = pltpu.roll(moved, (k * cap - 128 * t) % 128, 1)
            lane = jnp.where((column >= start) & (column < end), moved, lane)
        place[:, t * 128 : (t + 1) * 128] = onehot(iota((rows, 128), 0).astype(F32) == lane[0:1])
    total = jnp.zeros((rows, width), F32)
    for c in range(spaces // group):
        for k in range(max(1, c * group), (c + 1) * group):
            row_copy(k).wait_recv()
        arrived = recv[c * group : (c + 1) * group].reshape(group * cap, width)
        total = total + dot(place[:, c * group * cap : (c + 1) * group * cap], arrived)
    reg[...] = total.astype(BF16)

    def wait_sent(k, carry):
        row_copy(k).wait_send()
        return carry

    lax.fori_loop(1, spaces, wait_sent, 0)
    for copy in halos:
        copy.wait_send()


def front(features, neighbours, order, weight):
    spaces = lax.axis_size("space")
    rows, width = features.shape
    cap = 3 * rows // (2 * spaces)
    bricks = rows // EDGE**3
    face = EDGE * EDGE
    vmem = pl.BlockSpec(memory_space=pltpu.VMEM)
    return pl.pallas_call(
        functools.partial(front_kernel, spaces, cap),
        out_shape=[jax.ShapeDtypeStruct((rows, width), BF16)] * 2,
        in_specs=[vmem, pl.BlockSpec(memory_space=pltpu.SMEM), vmem, pl.BlockSpec(memory_space=pl.ANY)],
        out_specs=[vmem, vmem],
        scratch_shapes=[
            pltpu.VMEM(weight.shape, BF16),
            pltpu.VMEM((bricks, (EDGE + 2) * face, 9 * width), BF16),
            pltpu.VMEM((bricks, face, width), BF16),
            pltpu.VMEM((bricks, face, width), BF16),
            pltpu.VMEM((spaces, 8, 128), F32),
            pltpu.VMEM((spaces, 8, 128), F32),
            pltpu.VMEM((spaces, cap, width), BF16),
            pltpu.VMEM((spaces, cap, width), BF16),
            pltpu.VMEM((rows, spaces * cap), BF16),
            pltpu.SemaphoreType.DMA,
            pltpu.SemaphoreType.DMA((2 * bricks,)),
            pltpu.SemaphoreType.DMA((2 * bricks,)),
            pltpu.SemaphoreType.DMA((spaces,)),
            pltpu.SemaphoreType.DMA((spaces,)),
            pltpu.SemaphoreType.DMA((spaces,)),
            pltpu.SemaphoreType.DMA((spaces,)),
        ],
        compiler_params=pltpu.CompilerParams(collective_id=0, has_side_effects=True, vmem_limit_bytes=VMEM_LIMIT),
        cost_estimate=pl.CostEstimate(
            flops=2 * rows * 27 * width * width, bytes_accessed=weight.size * 2 + 6 * rows * width, transcendentals=0
        ),
        name="front",
    )(features, neighbours, order, weight)


def attention_kernel(
    spaces, reps, reg, wi, wo, cot, att, grad,
    q, k, v, ctx, s0, s1, *comm,
):
    chunks = [comm[n : n + 11] for n in range(0, len(comm), 11)]
    rows, width = reg.shape
    head = width // HEADS
    half = width // 2
    space, rep = lax.axis_index("space"), lax.axis_index("rep")
    planes, others = spaces // 2, 2 * reps
    chip, core = space // 2, space % 2
    place = rep * 2 + core

    def across(n):
        return {"space": lax.rem(chip + n, planes) * 2 + core}

    def along(n):
        there = lax.rem(place + n, others)
        return {"space": chip * 2 + there % 2, "rep": there // 2}

    def run(count, make):
        def body(n, carry):
            make(n)
            return carry

        lax.fori_loop(1, count, body, 0)

    barrier = pltpu.get_barrier_semaphore()
    run(planes, lambda n: pl.semaphore_signal(barrier, inc=1, device_id=across(n), device_id_type=MESH))
    run(others, lambda n: pl.semaphore_signal(barrier, inc=1, device_id=along(n), device_id_type=MESH))

    def copy(src, dst, send, recv, device):
        return pltpu.make_async_remote_copy(
            src_ref=src, dst_ref=dst, send_sem=send, recv_sem=recv, device_id=device, device_id_type=MESH
        )

    def scatter(c, n):
        term, first, part, second, final, s1, r1, s2, r2, s3, r3 = chunks[c]
        return copy(term.at[lax.rem(place + n, others)], first.at[n], s1.at[n], r1.at[n], along(n))

    def share(c, n, sender):
        term, first, part, second, final, s1, r1, s2, r2, s3, r3 = chunks[c]
        return copy(part, second.at[sender], s2.at[n], r2.at[n], across(n))

    def gather(c, n, sender):
        term, first, part, second, final, s1, r1, s2, r2, s3, r3 = chunks[c]
        return copy(final.at[sender], final.at[sender], s3.at[n], r3.at[n], along(n))

    def start_scatter(c, values):
        chunks[c][0][...] = values.reshape(chunks[c][0].shape)
        run(others, lambda n: scatter(c, n).start())

    def start_share(c):
        term, first, part, second = chunks[c][:4]
        first[0] = term[place]
        run(others, lambda n: scatter(c, n).wait())
        part[...] = jnp.sum(first[...], axis=0)
        run(planes, lambda n: share(c, n, chip).start())

    def start_gather(c):
        part, second, final = chunks[c][2:5]
        second[chip] = part[...]
        run(planes, lambda n: share(c, n, chip).wait_send())
        run(planes, lambda n: share(c, n, lax.rem(chip - n + planes, planes)).wait_recv())
        final[place] = jnp.sum(second[...], axis=0)
        run(others, lambda n: gather(c, n, place).start())

    def finish(c, at):
        final = chunks[c][4]
        run(others, lambda n: gather(c, n, place).wait_send())
        run(others, lambda n: gather(c, n, lax.rem(place - n + others, others)).wait_recv())
        grad[at] = final[...].reshape(-1, width)

    def gradient_rows(side):
        part_context = ctx[side].astype(BF16)
        return lax.dot_general(part_context, cot[...], (((0,), (0,)), ((), ())), preferred_element_type=F32)

    residual = reg[...].astype(F32)
    centred = residual - jnp.mean(residual, axis=-1, keepdims=True)
    variance = jnp.mean(centred * centred, axis=-1, keepdims=True)
    normed = (centred * lax.rsqrt(variance + 1e-05)).astype(BF16)
    packed = dot(normed, wi[...]).astype(BF16)
    q[...] = packed[:, :width] * jnp.asarray(head**-0.5, BF16)
    k[...] = packed[:, width : 2 * width]
    ones = jnp.ones((rows, half), BF16)
    for n in range(2):
        v[n] = jnp.concatenate([packed[:, 2 * width + n * half : 2 * width + (n + 1) * half], ones], axis=1)
    ctx[...] = jnp.zeros_like(ctx)
    tile = s0.shape[0]
    tiles = rows // tile
    lane_q = iota((tile, width), 1) // head
    lane_c = iota((tile, half), 1) // head
    held = (s0, s1)

    def scores(h, t):
        queries = jnp.where(lane_q == h, q[t * tile : (t + 1) * tile], jnp.zeros((), BF16))
        return dot_t(queries, k[...])

    def one_head(h):
        side = h // (HEADS // 2)
        for t in range(tiles):
            later = h if t < tiles - 1 else jnp.minimum(h + 1, HEADS - 1)
            held[(t + 1) % 2][...] = scores(later, (t + 1) % tiles)
            now = held[t % 2][...]
            lifted = jnp.exp(now - jnp.max(now, axis=-1, keepdims=True))
            both = dot(lifted.astype(BF16), v[side])
            at = slice(t * tile, (t + 1) * tile)
            ctx[side, at] += jnp.where(lane_c == h - side * (HEADS // 2), both[:, :half] / both[:, half:], 0.0)

    s0[...] = scores(0, 0)
    heads_a_step = HEADS // 4

    def step(n, carry):
        for m in range(heads_a_step):
            one_head(heads_a_step * n + m)

        @pl.when(n == 1)
        def _():
            values = gradient_rows(0)
            pl.semaphore_wait(barrier, planes + others - 2)
            start_scatter(0, values)

        @pl.when(n == 2)
        def _():
            start_scatter(1, gradient_rows(1)[: half // 2])
            start_share(0)

        return carry

    lax.fori_loop(0, 4, step, 0)
    start_scatter(2, gradient_rows(1)[half // 2 :])
    start_share(1)
    start_gather(0)
    context = jnp.concatenate([ctx[0], ctx[1]], axis=1).astype(BF16)
    att[...] = (reg[...].astype(F32) + dot(context, wo[...])).astype(BF16)
    start_share(2)
    start_gather(1)
    finish(0, slice(0, half))
    start_gather(2)
    finish(1, slice(half, half + half // 2))
    finish(2, slice(half + half // 2, width))


def attention(regrouped, wi, wo, cot):
    spaces, reps = lax.axis_size("space"), lax.axis_size("rep")
    rows, width = regrouped.shape
    half = width // 2
    planes, others = spaces // 2, 2 * reps
    tile = 256
    vmem = pl.BlockSpec(memory_space=pltpu.VMEM)
    dma = pltpu.SemaphoreType.DMA
    return pl.pallas_call(
        functools.partial(attention_kernel, spaces, reps),
        out_shape=[jax.ShapeDtypeStruct((rows, width), BF16), jax.ShapeDtypeStruct((width, width), F32)],
        in_specs=[vmem] * 4,
        out_specs=[vmem, vmem],
        scratch_shapes=[
            pltpu.VMEM((rows, width), BF16),
            pltpu.VMEM((rows, width), BF16),
            pltpu.VMEM((2, rows, width), BF16),
            pltpu.VMEM((2, rows, half), F32),
            pltpu.VMEM((tile, rows), F32),
            pltpu.VMEM((tile, rows), F32),
        ]
        + [
            spec
            for count in (half, half // 2, half // 2)
            for spec in (
                pltpu.VMEM((others, count // others, width), F32),
                pltpu.VMEM((others, count // others, width), F32),
                pltpu.VMEM((count // others, width), F32),
                pltpu.VMEM((planes, count // others, width), F32),
                pltpu.VMEM((others, count // others, width), F32),
                *[dma((others,))] * 2,
                *[dma((planes,))] * 2,
                *[dma((others,))] * 2,
            )
        ],
        compiler_params=pltpu.CompilerParams(collective_id=1, has_side_effects=True, vmem_limit_bytes=VMEM_LIMIT),
        cost_estimate=pl.CostEstimate(
            flops=4 * HEADS * rows * rows * width, bytes_accessed=8 * rows * width, transcendentals=HEADS * rows * rows
        ),
        name="attention",
    )(regrouped, wi, wo, cot)


def publish_kernel(count, *refs):
    given, made, held, sems = refs[:count], refs[count : 2 * count], refs[2 * count : 3 * count], refs[3 * count]
    reads = [pltpu.make_async_copy(given[n], held[n], sems.at[0, n]) for n in range(count)]
    writes = [pltpu.make_async_copy(held[n], made[n], sems.at[1, n]) for n in range(count)]
    for read in reads:
        read.start()
    for read, write in zip(reads, writes):
        read.wait()
        write.start()
    for write in writes:
        write.wait()


def publish(*arrays):
    spec = pl.BlockSpec(memory_space=pl.ANY)
    return pl.pallas_call(
        functools.partial(publish_kernel, len(arrays)),
        out_shape=[jax.ShapeDtypeStruct(a.shape, a.dtype) for a in arrays],
        in_specs=[spec] * len(arrays),
        out_specs=[spec] * len(arrays),
        scratch_shapes=[pltpu.VMEM(a.shape, a.dtype) for a in arrays] + [pltpu.SemaphoreType.DMA((2, len(arrays)))],
        name="publish",
    )(*arrays)


def local(features, neighbours, serial_order, kernel_weight, input_projection, output_projection, cotangent):
    encoded, regrouped = front(features[0], neighbours[0], serial_order, kernel_weight)
    attended, gradient = attention(regrouped, input_projection, output_projection, cotangent[0])
    encoded, attended, gradient = publish(encoded, attended, gradient)
    return encoded[None], attended[None], gradient


def solution(mesh):
    in_specs = (
        P("rep", "space", None),
        P("rep", "space", None),
        P("rep", "space"),
        P(),
        P(),
        P(),
        P("rep", "space", None),
    )
    out_specs = (P("rep", "space", None), P("rep", "space", None), P())
    return jax.shard_map(local, mesh=mesh, in_specs=in_specs, out_specs=out_specs, check_vma=False)
```

```python
import functools

import jax
import jax.numpy as jnp
from jax import lax
from jax.experimental import pallas as pl
from jax.experimental.pallas import tpu as pltpu
from jax.sharding import PartitionSpec as P

HEADS = 16
EDGE = 8
MESH = pl.DeviceIdType.MESH
F32 = jnp.float32
BF16 = jnp.bfloat16
VMEM_LIMIT = 60 * 1024 * 1024


def dot(a, b):
    return jnp.dot(a, b, preferred_element_type=F32)


def dot_t(a, b):
    return lax.dot_general(a, b, (((1,), (1,)), ((), ())), preferred_element_type=F32)


def iota(shape, dim):
    return lax.broadcasted_iota(jnp.int32, shape, dim)


def onehot(mask):
    return jnp.where(mask, 1.0, 0.0).astype(BF16)


def front_body(
    spaces, reps, cap, feat, nb, order, w_hbm, enc_out, enc, reg, enc_sem, loads,
    w, x, halo_l, halo_r, table, got, send, recv, place, picks, held,
    w_sem, hs, hr, ts, tr, rs, rr,
):
    me = lax.axis_index("space")
    rows, width = feat.shape
    face = EDGE * EDGE
    brick = EDGE * face
    bricks = rows // brick
    load = pltpu.make_async_copy(w_hbm, w, w_sem)
    load.start()
    for later in loads:
        later.start()

    def peer(k):
        return {"space": lax.rem(me + k, spaces)}

    barrier = pltpu.get_barrier_semaphore()

    def greet(k, carry):
        pl.semaphore_signal(barrier, inc=1, device_id=peer(k), device_id_type=MESH)
        return carry

    lax.fori_loop(1, spaces, greet, 0)
    rep = lax.axis_index("rep")
    for m in range(1, reps):
        for core in range(2):
            device = {"space": me // 2 * 2 + core, "rep": lax.rem(rep + m, reps)}
            pl.semaphore_signal(barrier, inc=1, device_id=device, device_id_type=MESH)

    depth = iota((EDGE + 2, EDGE, width), 1)

    def beside(b, offset, source_id):
        p, q, r = offset
        number = 9 * (p + 1) + 3 * (q + 1) + (r + 1)
        number -= number > 13
        target = nb[b, number]
        return jnp.where((target == source_id) & (target >= 0), 1.0, 0.0)

    def layer(ref, first):
        return ref[pl.ds(first, face)].astype(F32).reshape(EDGE, EDGE, width)

    def write_layer(b, i, p, sources, ids, own):
        grown = []
        for r in (-1, 0, 1):
            parts = []
            for q in (-1, 0, 1):
                part = slice(EDGE - 1, EDGE) if q < 0 else slice(0, 1) if q > 0 else slice(0, EDGE)
                if own is not None and q == 0 and r == 0:
                    parts.append(own)
                    continue
                total = None
                for source, one_id in zip(sources, ids):
                    term = source[part] * beside(b, (p, q, r), one_id)
                    total = term if total is None else total + term
                parts.append(total)
            grown.append(jnp.concatenate(parts, axis=0))
        below, here, above = grown
        variants = (
            pltpu.roll(jnp.where(depth == EDGE - 1, below, here), 1, 1),
            here,
            pltpu.roll(jnp.where(depth == 0, above, here), EDGE - 1, 1),
        )
        first = i * face if isinstance(i, int) else pl.multiple_of(i * face, face)
        for q in range(3):
            for r in range(3):
                n = 3 * q + r
                x[b, pl.ds(first, face), n * width : (n + 1) * width] = (
                    variants[r][q : q + EDGE].reshape(face, width).astype(BF16)
                )

    own_ids = [me * bricks + n for n in range(bricks)]
    left_ids = [(me - 1) * bricks + n for n in range(bricks)]
    right_ids = [(me + 1) * bricks + n for n in range(bricks)]

    def inner(i, carry):
        sources = [layer(feat, pl.multiple_of(n * brick + i * face, face)) for n in range(bricks)]
        for b in range(bricks):
            write_layer(b, i + 1, 0, sources, own_ids, sources[b])
        return carry

    lax.fori_loop(0, EDGE, inner, 0)

    places = order[...]
    shift = rows.bit_length() - 1
    owner = lax.shift_right_logical(places, shift)
    slot = places & (rows - 1)
    ahead = (owner - me + spaces) & (spaces - 1)
    chosen = jnp.where(iota((spaces, rows), 0) == ahead, 1.0, 0.0)
    before = onehot(iota((rows, rows), 0) < iota((rows, rows), 1))
    rank = jnp.sum(chosen * dot(chosen.astype(BF16), before), axis=0, keepdims=True)
    high = lax.shift_right_logical(slot, 5).astype(F32)
    low = (slot & 31).astype(F32)
    lanes = table.shape[2]
    by_rank = onehot(iota((lanes, rows), 0).astype(F32) == rank)
    stacked = jnp.concatenate([chosen * high, chosen * low, chosen], axis=0).astype(BF16)
    found = dot_t(stacked, by_rank)
    slots = found[:spaces] * 32.0 + found[spaces : 2 * spaces]
    slots = jnp.where(found[2 * spaces :] > 0.5, slots, -1.0)
    table[...] = jnp.broadcast_to(slots[:, None, :], table.shape)
    row_at = ahead.astype(F32) * float(cap) + rank

    pl.semaphore_wait(barrier, spaces - 1 + 2 * (reps - 1))

    halos = []
    for b in range(bricks):
        for source, dst, step, n in (
            (b * brick + brick - face, halo_l, 1, 2 * b),
            (b * brick, halo_r, spaces - 1, 2 * b + 1),
        ):
            copy = pltpu.make_async_remote_copy(
                src_ref=feat.at[pl.ds(source, face)], dst_ref=dst.at[b], send_sem=hs.at[n], recv_sem=hr.at[n],
                device_id=peer(step), device_id_type=MESH,
            )
            copy.start()
            halos.append(copy)

    def table_copy(k):
        return pltpu.make_async_remote_copy(
            src_ref=table.at[k], dst_ref=got.at[k], send_sem=ts.at[k], recv_sem=tr.at[k],
            device_id=peer(k), device_id_type=MESH,
        )

    def row_copy(k):
        return pltpu.make_async_remote_copy(
            src_ref=send.at[k], dst_ref=recv.at[k], send_sem=rs.at[k], recv_sem=rr.at[k],
            device_id=peer(k), device_id_type=MESH,
        )

    def start_table(k, carry):
        table_copy(k).start()
        return carry

    lax.fori_loop(1, spaces, start_table, 0)

    load.wait()
    tile = brick // 2
    group = 8

    def product(n, p):
        b, half = n // 2, n % 2
        first = pl.multiple_of(half * tile + p * face, face)
        return dot(x[b, pl.ds(first, tile), :], w[pl.ds(9 * p, 9)].reshape(9 * width, width))

    def conv_first(n, carry):
        held[n] = product(n, 1) + product(n, 2 - 2 * (n % 2))
        wanted = (iota((group * cap, rows), 0) + n * group * cap).astype(F32)
        picks[pl.ds(pl.multiple_of(n * group * cap, 128), group * cap)] = onehot(wanted == row_at)
        return carry

    lax.fori_loop(0, spaces // group, conv_first, 0)
    for copy in halos:
        copy.wait_recv()
    tops = [layer(feat, n * brick + brick - face) for n in range(bricks)]
    bottoms = [layer(feat, n * brick) for n in range(bricks)]
    lefts = [layer(halo_l.at[n], 0) for n in range(bricks)]
    rights = [layer(halo_r.at[n], 0) for n in range(bricks)]
    for b in range(bricks):
        write_layer(b, 0, -1, lefts + tops, left_ids + own_ids, None)
        write_layer(b, EDGE + 1, 1, bottoms + rights, own_ids + right_ids, None)

    def conv_last(n, carry):
        at = pl.ds(pl.multiple_of(n * tile, tile), tile)
        enc[at] = (feat[at].astype(F32) + held[n] + product(n, 2 * (n % 2))).astype(BF16)
        return carry

    lax.fori_loop(0, rows // tile, conv_last, 0)
    pltpu.make_async_copy(enc, enc_out, enc_sem).start()

    for c in range(spaces // group):
        block = dot(picks[c * group * cap : (c + 1) * group * cap], enc[...]).astype(BF16)
        send[c * group : (c + 1) * group] = block.reshape(group, cap, width)
        for k in range(max(1, c * group), (c + 1) * group):
            row_copy(k).start()
    recv[0] = send[0]
    got[0] = table[0]

    def wait_table(k, carry):
        table_copy(k).wait()
        return carry

    lax.fori_loop(1, spaces, wait_table, 0)
    column = iota((8, 128), 1)
    for t in range(spaces * cap // 128):
        lane = jnp.full((8, 128), -1.0, F32)
        for k in range(spaces):
            start, end = max(0, k * cap - 128 * t), min(128, (k + 1) * cap - 128 * t)
            if start >= end:
                continue
            moved = got[k]
            if (k * cap - 128 * t) % 128:
                moved = pltpu.roll(moved, (k * cap - 128 * t) % 128, 1)
            lane = jnp.where((column >= start) & (column < end), moved, lane)
        place[:, t * 128 : (t + 1) * 128] = onehot(iota((rows, 128), 0).astype(F32) == lane[0:1])
    total = jnp.zeros((rows, width), F32)
    for c in range(spaces // group):
        for k in range(max(1, c * group), (c + 1) * group):
            row_copy(k).wait_recv()
        arrived = recv[c * group : (c + 1) * group].reshape(group * cap, width)
        total = total + dot(place[:, c * group * cap : (c + 1) * group * cap], arrived)
    reg[...] = total.astype(BF16)

    def wait_sent(k, carry):
        row_copy(k).wait_send()
        return carry

    lax.fori_loop(1, spaces, wait_sent, 0)
    for copy in halos:
        copy.wait_send()


def attention_body(
    spaces, reps, reg, wi, wo, cot, att_out, att, grad, loads, att_sem,
    q, k, v, ctx, s0, s1, *comm,
):
    chunks = [comm[n : n + 11] for n in range(0, len(comm), 11)]
    rows, width = reg.shape
    head = width // HEADS
    half = width // 2
    space, rep = lax.axis_index("space"), lax.axis_index("rep")
    planes, others = spaces // 2, 2 * reps
    chip, core = space // 2, space % 2
    place = rep * 2 + core

    def across(n):
        return {"space": lax.rem(chip + n, planes) * 2 + core}

    def along(n):
        there = lax.rem(place + n, others)
        return {"space": chip * 2 + there % 2, "rep": there // 2}

    def run(count, make):
        def body(n, carry):
            make(n)
            return carry

        lax.fori_loop(1, count, body, 0)

    def copy(src, dst, send, recv, device):
        return pltpu.make_async_remote_copy(
            src_ref=src, dst_ref=dst, send_sem=send, recv_sem=recv, device_id=device, device_id_type=MESH
        )

    def scatter(c, n):
        term, first, part, second, final, s1, r1, s2, r2, s3, r3 = chunks[c]
        return copy(term.at[lax.rem(place + n, others)], first.at[n], s1.at[n], r1.at[n], along(n))

    def share(c, n, sender):
        term, first, part, second, final, s1, r1, s2, r2, s3, r3 = chunks[c]
        return copy(part, second.at[sender], s2.at[n], r2.at[n], across(n))

    def gather(c, n, sender):
        term, first, part, second, final, s1, r1, s2, r2, s3, r3 = chunks[c]
        return copy(final.at[sender], final.at[sender], s3.at[n], r3.at[n], along(n))

    def start_scatter(c, values):
        chunks[c][0][...] = values.reshape(chunks[c][0].shape)
        run(others, lambda n: scatter(c, n).start())

    def start_share(c):
        term, first, part, second = chunks[c][:4]
        first[0] = term[place]
        run(others, lambda n: scatter(c, n).wait())
        part[...] = jnp.sum(first[...], axis=0)
        run(planes, lambda n: share(c, n, chip).start())

    def start_gather(c):
        part, second, final = chunks[c][2:5]
        second[chip] = part[...]
        run(planes, lambda n: share(c, n, chip).wait_send())
        run(planes, lambda n: share(c, n, lax.rem(chip - n + planes, planes)).wait_recv())
        final[place] = jnp.sum(second[...], axis=0)
        run(others, lambda n: gather(c, n, place).start())

    def finish(c, at):
        final = chunks[c][4]
        run(others, lambda n: gather(c, n, place).wait_send())
        run(others, lambda n: gather(c, n, lax.rem(place - n + others, others)).wait_recv())
        grad[at] = final[...].reshape(-1, width)

    def gradient_rows(side):
        part_context = ctx[side].astype(BF16)
        return lax.dot_general(part_context, cot[...], (((0,), (0,)), ((), ())), preferred_element_type=F32)

    for load in loads:
        load.wait()
    residual = reg[...].astype(F32)
    centred = residual - jnp.mean(residual, axis=-1, keepdims=True)
    variance = jnp.mean(centred * centred, axis=-1, keepdims=True)
    normed = (centred * lax.rsqrt(variance + 1e-05)).astype(BF16)
    packed = dot(normed, wi[...]).astype(BF16)
    q[...] = packed[:, :width] * jnp.asarray(head**-0.5, BF16)
    k[...] = packed[:, width : 2 * width]
    ones = jnp.ones((rows, half), BF16)
    for n in range(2):
        v[n] = jnp.concatenate([packed[:, 2 * width + n * half : 2 * width + (n + 1) * half], ones], axis=1)
    ctx[...] = jnp.zeros_like(ctx)
    tile = s0.shape[0]
    tiles = rows // tile
    lane_q = iota((tile, width), 1) // head
    lane_c = iota((tile, half), 1) // head
    held = (s0, s1)

    def scores(h, t):
        queries = jnp.where(lane_q == h, q[t * tile : (t + 1) * tile], jnp.zeros((), BF16))
        return dot_t(queries, k[...])

    def one_head(h):
        side = h // (HEADS // 2)
        for t in range(tiles):
            later = h if t < tiles - 1 else jnp.minimum(h + 1, HEADS - 1)
            held[(t + 1) % 2][...] = scores(later, (t + 1) % tiles)
            now = held[t % 2][...]
            lifted = jnp.exp(now - jnp.max(now, axis=-1, keepdims=True))
            both = dot(lifted.astype(BF16), v[side])
            at = slice(t * tile, (t + 1) * tile)
            ctx[side, at] += jnp.where(lane_c == h - side * (HEADS // 2), both[:, :half] / both[:, half:], 0.0)

    s0[...] = scores(0, 0)
    heads_a_step = HEADS // 4

    def step(n, carry):
        for m in range(heads_a_step):
            one_head(heads_a_step * n + m)

        @pl.when(n == 1)
        def _():
            start_scatter(0, gradient_rows(0))

        @pl.when(n == 2)
        def _():
            start_scatter(1, gradient_rows(1)[: half // 2])
            start_share(0)

        return carry

    lax.fori_loop(0, 4, step, 0)
    start_scatter(2, gradient_rows(1)[half // 2 :])
    start_share(1)
    start_gather(0)
    context = jnp.concatenate([ctx[0], ctx[1]], axis=1).astype(BF16)
    att[...] = (reg[...].astype(F32) + dot(context, wo[...])).astype(BF16)
    pltpu.make_async_copy(att, att_out, att_sem).start()
    start_share(2)
    start_gather(1)
    finish(0, slice(0, half))
    start_gather(2)
    finish(1, slice(half, half + half // 2))
    finish(2, slice(half + half // 2, width))


def layer_kernel(spaces, reps, cap, feat, nb, order, *refs):
    w_hbm, wi_hbm, wo_hbm, cot_hbm, enc_out, att_out, grad_out = refs[:7]
    wi, wo, cot, enc, reg, att, grad, sems = refs[7:15]
    front_refs, attention_refs = refs[15:33], refs[33:]
    loads = [
        pltpu.make_async_copy(source, held, sems.at[n])
        for n, (source, held) in enumerate(((wi_hbm, wi), (wo_hbm, wo), (cot_hbm, cot)))
    ]
    front_body(spaces, reps, cap, feat, nb, order, w_hbm, enc_out, enc, reg, sems.at[3], loads, *front_refs)
    attention_body(spaces, reps, reg, wi, wo, cot, att_out, att, grad, loads, sems.at[4], *attention_refs)
    last = pltpu.make_async_copy(grad, grad_out, sems.at[5])
    last.start()
    pltpu.make_async_copy(enc, enc_out, sems.at[3]).wait()
    pltpu.make_async_copy(att, att_out, sems.at[4]).wait()
    last.wait()


def layer(features, neighbours, order, weight, wi, wo, cot):
    spaces, reps = lax.axis_size("space"), lax.axis_size("rep")
    rows, width = features.shape
    cap = 3 * rows // (2 * spaces)
    bricks = rows // EDGE**3
    face = EDGE * EDGE
    half = width // 2
    planes, others = spaces // 2, 2 * reps
    tile = 256
    vmem = pl.BlockSpec(memory_space=pltpu.VMEM)
    hbm = pl.BlockSpec(memory_space=pl.ANY)
    dma = pltpu.SemaphoreType.DMA
    full = pltpu.VMEM((rows, width), BF16)
    shared = [
        pltpu.VMEM(wi.shape, BF16),
        pltpu.VMEM(wo.shape, BF16),
        *[full] * 4,
        pltpu.VMEM((width, width), F32),
        dma((6,)),
    ]
    for_front = [
        pltpu.VMEM(weight.shape, BF16),
        pltpu.VMEM((bricks, (EDGE + 2) * face, 9 * width), BF16),
        pltpu.VMEM((bricks, face, width), BF16),
        pltpu.VMEM((bricks, face, width), BF16),
        pltpu.VMEM((spaces, 8, 128), F32),
        pltpu.VMEM((spaces, 8, 128), F32),
        pltpu.VMEM((spaces, cap, width), BF16),
        pltpu.VMEM((spaces, cap, width), BF16),
        pltpu.VMEM((rows, spaces * cap), BF16),
        pltpu.VMEM((spaces * cap, rows), BF16),
        pltpu.VMEM((2 * bricks, EDGE**3 // 2, width), F32),
        dma,
        dma((2 * bricks,)),
        dma((2 * bricks,)),
        *[dma((spaces,))] * 4,
    ]
    for_attention = [
        full,
        full,
        pltpu.VMEM((2, rows, width), BF16),
        pltpu.VMEM((2, rows, half), F32),
        pltpu.VMEM((tile, rows), F32),
        pltpu.VMEM((tile, rows), F32),
    ]
    for count in (half, half // 2, half // 2):
        for_attention += [
            pltpu.VMEM((others, count // others, width), F32),
            pltpu.VMEM((others, count // others, width), F32),
            pltpu.VMEM((count // others, width), F32),
            pltpu.VMEM((planes, count // others, width), F32),
            pltpu.VMEM((others, count // others, width), F32),
            *[dma((others,))] * 2,
            *[dma((planes,))] * 2,
            *[dma((others,))] * 2,
        ]
    return pl.pallas_call(
        functools.partial(layer_kernel, spaces, reps, cap),
        out_shape=[
            jax.ShapeDtypeStruct((rows, width), BF16),
            jax.ShapeDtypeStruct((rows, width), BF16),
            jax.ShapeDtypeStruct((width, width), F32),
        ],
        in_specs=[vmem, pl.BlockSpec(memory_space=pltpu.SMEM), vmem, hbm, hbm, hbm, hbm],
        out_specs=[hbm] * 3,
        scratch_shapes=shared + for_front + for_attention,
        compiler_params=pltpu.CompilerParams(collective_id=0, has_side_effects=True, vmem_limit_bytes=VMEM_LIMIT),
        cost_estimate=pl.CostEstimate(
            flops=2 * rows * 27 * width * width + 4 * HEADS * rows * rows * width,
            bytes_accessed=weight.size * 2 + 12 * rows * width,
            transcendentals=HEADS * rows * rows,
        ),
        name="layer",
    )(features, neighbours, order, weight, wi, wo, cot)


def publish_kernel(count, *refs):
    given, made, held, sems = refs[:count], refs[count : 2 * count], refs[2 * count : 3 * count], refs[3 * count]
    reads = [pltpu.make_async_copy(given[n], held[n], sems.at[0, n]) for n in range(count)]
    writes = [pltpu.make_async_copy(held[n], made[n], sems.at[1, n]) for n in range(count)]
    for read in reads:
        read.start()
    for read, write in zip(reads, writes):
        read.wait()
        write.start()
    for write in writes:
        write.wait()


def publish(*arrays):
    spec = pl.BlockSpec(memory_space=pl.ANY)
    return pl.pallas_call(
        functools.partial(publish_kernel, len(arrays)),
        out_shape=[jax.ShapeDtypeStruct(a.shape, a.dtype) for a in arrays],
        in_specs=[spec] * len(arrays),
        out_specs=[spec] * len(arrays),
        scratch_shapes=[pltpu.VMEM(a.shape, a.dtype) for a in arrays] + [pltpu.SemaphoreType.DMA((2, len(arrays)))],
        name="publish",
    )(*arrays)


def local(features, neighbours, serial_order, kernel_weight, input_projection, output_projection, cotangent):
    results = layer(
        features[0], neighbours[0], serial_order, kernel_weight, input_projection, output_projection, cotangent[0]
    )
    encoded, attended, gradient = publish(*results)
    return encoded[None], attended[None], gradient


def solution(mesh):
    in_specs = (
        P("rep", "space", None),
        P("rep", "space", None),
        P("rep", "space"),
        P(),
        P(),
        P(),
        P("rep", "space", None),
    )
    out_specs = (P("rep", "space", None), P("rep", "space", None), P())
    return jax.shard_map(local, mesh=mesh, in_specs=in_specs, out_specs=out_specs, check_vma=False)
```

```python
import functools

import jax
import jax.numpy as jnp
from jax import lax
from jax.experimental import pallas as pl
from jax.experimental.pallas import tpu as pltpu
from jax.sharding import PartitionSpec as P

HEADS = 16
EDGE = 8
MESH = pl.DeviceIdType.MESH
F32 = jnp.float32
BF16 = jnp.bfloat16
VMEM_LIMIT = 60 * 1024 * 1024


def dot(a, b):
    return jnp.dot(a, b, preferred_element_type=F32)


def dot_t(a, b):
    return lax.dot_general(a, b, (((1,), (1,)), ((), ())), preferred_element_type=F32)


def iota(shape, dim):
    return lax.broadcasted_iota(jnp.int32, shape, dim)


def onehot(mask):
    return jnp.where(mask, 1.0, 0.0).astype(BF16)


def front_body(
    spaces, reps, cap, feat, nb, order, w_hbm, enc_out, enc, reg, enc_sem, loads, meanwhile,
    w, x, halo_l, halo_r, table, passed, got, send, recv, place, picks, held,
    w_sem, hs, hr, ts, tr, us, ur, rs, rr,
):
    me = lax.axis_index("space")
    rows, width = feat.shape
    face = EDGE * EDGE
    brick = EDGE * face
    bricks = rows // brick
    outer, inner = got.shape[:2]
    line, within = me // inner, lax.rem(me, inner)
    load = pltpu.make_async_copy(w_hbm, w, w_sem)
    load.start()
    for later in loads:
        later.start()

    def peer(k):
        return {"space": lax.rem(me + k, spaces)}

    barrier = pltpu.get_barrier_semaphore()

    def greet(k, carry):
        pl.semaphore_signal(barrier, inc=1, device_id=peer(k), device_id_type=MESH)
        return carry

    lax.fori_loop(1, spaces, greet, 0)
    rep = lax.axis_index("rep")
    for m in range(1, reps):
        for core in range(2):
            device = {"space": me // 2 * 2 + core, "rep": lax.rem(rep + m, reps)}
            pl.semaphore_signal(barrier, inc=1, device_id=device, device_id_type=MESH)

    depth = iota((EDGE + 2, EDGE, width), 1)

    def beside(b, offset, source_id):
        p, q, r = offset
        number = 9 * (p + 1) + 3 * (q + 1) + (r + 1)
        number -= number > 13
        target = nb[b, number]
        return jnp.where((target == source_id) & (target >= 0), 1.0, 0.0)

    def layer(ref, first):
        return ref[pl.ds(first, face)].astype(F32).reshape(EDGE, EDGE, width)

    def write_layer(b, i, p, sources, ids, own):
        grown = []
        for r in (-1, 0, 1):
            parts = []
            for q in (-1, 0, 1):
                part = slice(EDGE - 1, EDGE) if q < 0 else slice(0, 1) if q > 0 else slice(0, EDGE)
                if own is not None and q == 0 and r == 0:
                    parts.append(own)
                    continue
                total = None
                for source, one_id in zip(sources, ids):
                    term = source[part] * beside(b, (p, q, r), one_id)
                    total = term if total is None else total + term
                parts.append(total)
            grown.append(jnp.concatenate(parts, axis=0))
        below, here, above = grown
        variants = (
            pltpu.roll(jnp.where(depth == EDGE - 1, below, here), 1, 1),
            here,
            pltpu.roll(jnp.where(depth == 0, above, here), EDGE - 1, 1),
        )
        first = (i * bricks + b) * face
        first = first if isinstance(first, int) else pl.multiple_of(first, face)
        for q in range(3):
            for r in range(3):
                n = 3 * q + r
                x[pl.ds(first, face), n * width : (n + 1) * width] = (
                    variants[r][q : q + EDGE].reshape(face, width).astype(BF16)
                )

    own_ids = [me * bricks + n for n in range(bricks)]
    left_ids = [(me - 1) * bricks + n for n in range(bricks)]
    right_ids = [(me + 1) * bricks + n for n in range(bricks)]

    def inner_layer(i, carry):
        sources = [layer(feat, pl.multiple_of(n * brick + i * face, face)) for n in range(bricks)]
        for b in range(bricks):
            write_layer(b, i + 1, 0, sources, own_ids, sources[b])
        return carry

    lax.fori_loop(0, EDGE, inner_layer, 0)

    places = order[...]
    shift = rows.bit_length() - 1
    owner = lax.shift_right_logical(places, shift)
    slot = places & (rows - 1)
    ahead = (owner - me + spaces) & (spaces - 1)
    chosen = jnp.where(iota((spaces, rows), 0) == owner, 1.0, 0.0)
    before = onehot(iota((rows, rows), 0) < iota((rows, rows), 1))
    rank = jnp.sum(chosen * dot(chosen.astype(BF16), before), axis=0, keepdims=True)
    high = lax.shift_right_logical(slot, 5).astype(F32)
    low = (slot & 31).astype(F32)
    lanes = table.shape[3]
    by_rank = onehot(iota((lanes, rows), 0).astype(F32) == rank)
    stacked = jnp.concatenate([chosen * high, chosen * low, chosen], axis=0).astype(BF16)
    found = dot_t(stacked, by_rank)
    slots = found[:spaces] * 32.0 + found[spaces : 2 * spaces]
    slots = jnp.where(found[2 * spaces :] > 0.5, slots, -1.0)
    for n in range(outer):
        table[:, n] = jnp.broadcast_to(slots[n * inner : (n + 1) * inner][:, None, :], (inner, 8, lanes))
    row_at = ahead.astype(F32) * float(cap) + rank

    pl.semaphore_wait(barrier, spaces - 1 + 2 * (reps - 1))

    halos = []
    for b in range(bricks):
        for source, dst, step, n in (
            (b * brick + brick - face, halo_l, 1, 2 * b),
            (b * brick, halo_r, spaces - 1, 2 * b + 1),
        ):
            copy = pltpu.make_async_remote_copy(
                src_ref=feat.at[pl.ds(source, face)], dst_ref=dst.at[b], send_sem=hs.at[n], recv_sem=hr.at[n],
                device_id=peer(step), device_id_type=MESH,
            )
            copy.start()
            halos.append(copy)

    def inner_table(n, sender):
        return pltpu.make_async_remote_copy(
            src_ref=table.at[lax.rem(within + n, inner)], dst_ref=passed.at[sender], send_sem=ts.at[n], recv_sem=tr.at[n],
            device_id={"space": line * inner + lax.rem(within + n, inner)}, device_id_type=MESH,
        )

    def outer_table(n, sender):
        there = lax.rem(line + n, outer)
        return pltpu.make_async_remote_copy(
            src_ref=passed.at[:, there], dst_ref=got.at[sender], send_sem=us.at[n], recv_sem=ur.at[n],
            device_id={"space": there * inner + within}, device_id_type=MESH,
        )

    def row_copy(k):
        return pltpu.make_async_remote_copy(
            src_ref=send.at[k], dst_ref=recv.at[k], send_sem=rs.at[k], recv_sem=rr.at[k],
            device_id=peer(k), device_id_type=MESH,
        )

    for n in range(1, inner):
        inner_table(n, within).start()

    load.wait()
    halves = EDGE // 2
    block = halves * bricks * face
    group = 8

    def product(n, p):
        first = pl.multiple_of((n * halves + p) * bricks * face, face)
        return dot(x[pl.ds(first, block), :], w[pl.ds(9 * p, 9)].reshape(9 * width, width))

    def conv_first(n, carry):
        held[n] = product(n, 1) + product(n, 2 - 2 * n)
        part = spaces * cap // 2
        wanted = (iota((part, rows), 0) + n * part).astype(F32)
        picks[pl.ds(pl.multiple_of(n * part, 128), part)] = onehot(wanted == row_at)
        return carry

    lax.fori_loop(0, 2, conv_first, 0)
    passed[within] = table[within]
    for n in range(1, inner):
        inner_table(n, within).wait_send()
        inner_table(n, lax.rem(within - n + inner, inner)).wait_recv()
    for n in range(1, outer):
        outer_table(n, line).start()
    for copy in halos:
        copy.wait_recv()
    tops = [layer(feat, n * brick + brick - face) for n in range(bricks)]
    bottoms = [layer(feat, n * brick) for n in range(bricks)]
    lefts = [layer(halo_l.at[n], 0) for n in range(bricks)]
    rights = [layer(halo_r.at[n], 0) for n in range(bricks)]
    for b in range(bricks):
        write_layer(b, 0, -1, lefts + tops, left_ids + own_ids, None)
        write_layer(b, EDGE + 1, 1, bottoms + rights, own_ids + right_ids, None)

    def conv_last(n, carry):
        total = held[n] + product(n, 2 * n)
        for i in range(halves):
            for b in range(bricks):
                at = pl.ds(pl.multiple_of(b * brick + (n * halves + i) * face, face), face)
                rows_in = (i * bricks + b) * face
                enc[at] = (feat[at].astype(F32) + total[rows_in : rows_in + face]).astype(BF16)
        return carry

    lax.fori_loop(0, 2, conv_last, 0)
    pltpu.make_async_copy(enc, enc_out, enc_sem).start()

    for c in range(spaces // group):
        block = dot(picks[c * group * cap : (c + 1) * group * cap], enc[...]).astype(BF16)
        send[c * group : (c + 1) * group] = block.reshape(group, cap, width)
        for k in range(max(1, c * group), (c + 1) * group):
            row_copy(k).start()
    recv[0] = send[0]
    meanwhile()
    for n in range(inner):
        got[line, n] = passed[n, line]
    for n in range(1, outer):
        outer_table(n, line).wait_send()
        outer_table(n, lax.rem(line - n + outer, outer)).wait_recv()
    column = iota((8, 128), 1)
    for t in range(spaces * cap // 128):
        lane = jnp.full((8, 128), -1.0, F32)
        for k in range(spaces):
            start, end = max(0, k * cap - 128 * t), min(128, (k + 1) * cap - 128 * t)
            if start >= end:
                continue
            source = lax.rem(me - k + spaces, spaces)
            moved = got[source // inner, lax.rem(source, inner)]
            if (k * cap - 128 * t) % 128:
                moved = pltpu.roll(moved, (k * cap - 128 * t) % 128, 1)
            lane = jnp.where((column >= start) & (column < end), moved, lane)
        place[:, t * 128 : (t + 1) * 128] = onehot(iota((rows, 128), 0).astype(F32) == lane[0:1])
    total = jnp.zeros((rows, width), F32)
    for c in range(spaces // group):
        for k in range(max(1, c * group), (c + 1) * group):
            row_copy(k).wait_recv()
        arrived = recv[c * group : (c + 1) * group].reshape(group * cap, width)
        total = total + dot(place[:, c * group * cap : (c + 1) * group * cap], arrived)
    reg[...] = total.astype(BF16)

    def wait_sent(k, carry):
        row_copy(k).wait_send()
        return carry

    lax.fori_loop(1, spaces, wait_sent, 0)
    for copy in halos:
        copy.wait_send()


def attention_body(
    spaces, reps, reg, wi, wo, cot, att_out, att, grad, loads, att_sem,
    q, k, v, ctx, s0, s1, *comm,
):
    chunks = [comm[n : n + 11] for n in range(0, len(comm), 11)]
    rows, width = reg.shape
    head = width // HEADS
    half = width // 2
    space, rep = lax.axis_index("space"), lax.axis_index("rep")
    planes, others = spaces // 2, 2 * reps
    chip, core = space // 2, space % 2
    place = rep * 2 + core

    def across(n):
        return {"space": lax.rem(chip + n, planes) * 2 + core}

    def along(n):
        there = lax.rem(place + n, others)
        return {"space": chip * 2 + there % 2, "rep": there // 2}

    def run(count, make):
        def body(n, carry):
            make(n)
            return carry

        lax.fori_loop(1, count, body, 0)

    def copy(src, dst, send, recv, device):
        return pltpu.make_async_remote_copy(
            src_ref=src, dst_ref=dst, send_sem=send, recv_sem=recv, device_id=device, device_id_type=MESH
        )

    def scatter(c, n):
        term, first, part, second, final, s1, r1, s2, r2, s3, r3 = chunks[c]
        return copy(term.at[lax.rem(place + n, others)], first.at[n], s1.at[n], r1.at[n], along(n))

    def share(c, n, sender):
        term, first, part, second, final, s1, r1, s2, r2, s3, r3 = chunks[c]
        return copy(part, second.at[sender], s2.at[n], r2.at[n], across(n))

    def gather(c, n, sender):
        term, first, part, second, final, s1, r1, s2, r2, s3, r3 = chunks[c]
        return copy(final.at[sender], final.at[sender], s3.at[n], r3.at[n], along(n))

    def start_scatter(c, values):
        chunks[c][0][...] = values.reshape(chunks[c][0].shape)
        run(others, lambda n: scatter(c, n).start())

    def start_share(c):
        term, first, part, second = chunks[c][:4]
        first[0] = term[place]
        run(others, lambda n: scatter(c, n).wait())
        part[...] = jnp.sum(first[...], axis=0)
        run(planes, lambda n: share(c, n, chip).start())

    def start_gather(c):
        part, second, final = chunks[c][2:5]
        second[chip] = part[...]
        run(planes, lambda n: share(c, n, chip).wait_send())
        run(planes, lambda n: share(c, n, lax.rem(chip - n + planes, planes)).wait_recv())
        final[place] = jnp.sum(second[...], axis=0)
        run(others, lambda n: gather(c, n, place).start())

    def finish(c, at):
        final = chunks[c][4]
        run(others, lambda n: gather(c, n, place).wait_send())
        run(others, lambda n: gather(c, n, lax.rem(place - n + others, others)).wait_recv())
        grad[at] = final[...].reshape(-1, width)

    def gradient_rows(side):
        part_context = ctx[side].astype(BF16)
        return lax.dot_general(part_context, cot[...], (((0,), (0,)), ((), ())), preferred_element_type=F32)

    for load in loads:
        load.wait()
    residual = reg[...].astype(F32)
    centred = residual - jnp.mean(residual, axis=-1, keepdims=True)
    variance = jnp.mean(centred * centred, axis=-1, keepdims=True)
    normed = (centred * lax.rsqrt(variance + 1e-05)).astype(BF16)
    packed = dot(normed, wi[...]).astype(BF16)
    q[...] = packed[:, :width] * jnp.asarray(head**-0.5, BF16)
    k[...] = packed[:, width : 2 * width]
    for n in range(2):
        v[n, :, :half] = packed[:, 2 * width + n * half : 2 * width + (n + 1) * half]
    tile = s0.shape[0]
    tiles = rows // tile
    lane_q = iota((tile, width), 1) // head
    lane_c = iota((tile, half), 1) // head
    held = (s0, s1)

    def scores(h, t):
        queries = jnp.where(lane_q == h, q[t * tile : (t + 1) * tile], jnp.zeros((), BF16))
        return dot_t(queries, k[...])

    def one_head(h):
        side = h // (HEADS // 2)
        for t in range(tiles):
            later = h if t < tiles - 1 else jnp.minimum(h + 1, HEADS - 1)
            held[(t + 1) % 2][...] = scores(later, (t + 1) % tiles)
            now = held[t % 2][...]
            lifted = jnp.exp(now - jnp.max(now, axis=-1, keepdims=True))
            both = dot(lifted.astype(BF16), v[side])
            at = slice(t * tile, (t + 1) * tile)
            ctx[side, at] += jnp.where(lane_c == h - side * (HEADS // 2), both[:, :half] / both[:, half:], 0.0)

    s0[...] = scores(0, 0)
    heads_a_step = HEADS // 4

    def step(n, carry):
        for m in range(heads_a_step):
            one_head(heads_a_step * n + m)

        @pl.when(n == 1)
        def _():
            start_scatter(0, gradient_rows(0))

        @pl.when(n == 2)
        def _():
            start_scatter(1, gradient_rows(1)[: half // 2])
            start_share(0)

        return carry

    lax.fori_loop(0, 4, step, 0)
    start_scatter(2, gradient_rows(1)[half // 2 :])
    start_share(1)
    start_gather(0)
    context = jnp.concatenate([ctx[0], ctx[1]], axis=1).astype(BF16)
    att[...] = (reg[...].astype(F32) + dot(context, wo[...])).astype(BF16)
    pltpu.make_async_copy(att, att_out, att_sem).start()
    start_share(2)
    start_gather(1)
    finish(0, slice(0, half))
    start_gather(2)
    finish(1, slice(half, half + half // 2))
    finish(2, slice(half + half // 2, width))


def layer_kernel(spaces, reps, cap, feat, nb, order, *refs):
    w_hbm, wi_hbm, wo_hbm, cot_hbm, enc_out, att_out, grad_out = refs[:7]
    wi, wo, cot, enc, reg, att, grad, sems = refs[7:15]
    front_refs, attention_refs = refs[15:36], refs[36:]
    v, ctx = attention_refs[2:4]
    loads = [
        pltpu.make_async_copy(source, held, sems.at[n])
        for n, (source, held) in enumerate(((wi_hbm, wi), (wo_hbm, wo), (cot_hbm, cot)))
    ]

    def meanwhile():
        v[:, :, ctx.shape[2] :] = jnp.ones(ctx.shape, BF16)
        ctx[...] = jnp.zeros_like(ctx)

    front_body(spaces, reps, cap, feat, nb, order, w_hbm, enc_out, enc, reg, sems.at[3], loads, meanwhile, *front_refs)
    attention_body(spaces, reps, reg, wi, wo, cot, att_out, att, grad, loads, sems.at[4], *attention_refs)
    last = pltpu.make_async_copy(grad, grad_out, sems.at[5])
    last.start()
    pltpu.make_async_copy(enc, enc_out, sems.at[3]).wait()
    pltpu.make_async_copy(att, att_out, sems.at[4]).wait()
    last.wait()


def layer(features, neighbours, order, weight, wi, wo, cot):
    spaces, reps = lax.axis_size("space"), lax.axis_size("rep")
    rows, width = features.shape
    cap = 3 * rows // (2 * spaces)
    bricks = rows // EDGE**3
    face = EDGE * EDGE
    half = width // 2
    inner, outer = 8, spaces // 8
    planes, others = spaces // 2, 2 * reps
    tile = 256
    vmem = pl.BlockSpec(memory_space=pltpu.VMEM)
    hbm = pl.BlockSpec(memory_space=pl.ANY)
    dma = pltpu.SemaphoreType.DMA
    full = pltpu.VMEM((rows, width), BF16)
    shared = [
        pltpu.VMEM(wi.shape, BF16),
        pltpu.VMEM(wo.shape, BF16),
        *[full] * 4,
        pltpu.VMEM((width, width), F32),
        dma((6,)),
    ]
    for_front = [
        pltpu.VMEM(weight.shape, BF16),
        pltpu.VMEM(((EDGE + 2) * bricks * face, 9 * width), BF16),
        pltpu.VMEM((bricks, face, width), BF16),
        pltpu.VMEM((bricks, face, width), BF16),
        pltpu.VMEM((inner, outer, 8, 128), F32),
        pltpu.VMEM((inner, outer, 8, 128), F32),
        pltpu.VMEM((outer, inner, 8, 128), F32),
        pltpu.VMEM((spaces, cap, width), BF16),
        pltpu.VMEM((spaces, cap, width), BF16),
        pltpu.VMEM((rows, spaces * cap), BF16),
        pltpu.VMEM((spaces * cap, rows), BF16),
        pltpu.VMEM((2, rows // 2, width), F32),
        dma,
        dma((2 * bricks,)),
        dma((2 * bricks,)),
        *[dma((inner,))] * 2,
        *[dma((outer,))] * 2,
        *[dma((spaces,))] * 2,
    ]
    for_attention = [
        full,
        full,
        pltpu.VMEM((2, rows, width), BF16),
        pltpu.VMEM((2, rows, half), F32),
        pltpu.VMEM((tile, rows), F32),
        pltpu.VMEM((tile, rows), F32),
    ]
    for count in (half, half // 2, half // 2):
        for_attention += [
            pltpu.VMEM((others, count // others, width), F32),
            pltpu.VMEM((others, count // others, width), F32),
            pltpu.VMEM((count // others, width), F32),
            pltpu.VMEM((planes, count // others, width), F32),
            pltpu.VMEM((others, count // others, width), F32),
            *[dma((others,))] * 2,
            *[dma((planes,))] * 2,
            *[dma((others,))] * 2,
        ]
    return pl.pallas_call(
        functools.partial(layer_kernel, spaces, reps, cap),
        out_shape=[
            jax.ShapeDtypeStruct((rows, width), BF16),
            jax.ShapeDtypeStruct((rows, width), BF16),
            jax.ShapeDtypeStruct((width, width), F32),
        ],
        in_specs=[vmem, pl.BlockSpec(memory_space=pltpu.SMEM), vmem, hbm, hbm, hbm, hbm],
        out_specs=[hbm] * 3,
        scratch_shapes=shared + for_front + for_attention,
        compiler_params=pltpu.CompilerParams(collective_id=0, has_side_effects=True, vmem_limit_bytes=VMEM_LIMIT),
        cost_estimate=pl.CostEstimate(
            flops=2 * rows * 27 * width * width + 4 * HEADS * rows * rows * width,
            bytes_accessed=weight.size * 2 + 12 * rows * width,
            transcendentals=HEADS * rows * rows,
        ),
        name="layer",
    )(features, neighbours, order, weight, wi, wo, cot)


def publish_kernel(count, *refs):
    given, made, held, sems = refs[:count], refs[count : 2 * count], refs[2 * count : 3 * count], refs[3 * count]
    reads = [pltpu.make_async_copy(given[n], held[n], sems.at[0, n]) for n in range(count)]
    writes = [pltpu.make_async_copy(held[n], made[n], sems.at[1, n]) for n in range(count)]
    for read in reads:
        read.start()
    for read, write in zip(reads, writes):
        read.wait()
        write.start()
    for write in writes:
        write.wait()


def publish(*arrays):
    spec = pl.BlockSpec(memory_space=pl.ANY)
    return pl.pallas_call(
        functools.partial(publish_kernel, len(arrays)),
        out_shape=[jax.ShapeDtypeStruct(a.shape, a.dtype) for a in arrays],
        in_specs=[spec] * len(arrays),
        out_specs=[spec] * len(arrays),
        scratch_shapes=[pltpu.VMEM(a.shape, a.dtype) for a in arrays] + [pltpu.SemaphoreType.DMA((2, len(arrays)))],
        name="publish",
    )(*arrays)


def local(features, neighbours, serial_order, kernel_weight, input_projection, output_projection, cotangent):
    results = layer(
        features[0], neighbours[0], serial_order, kernel_weight, input_projection, output_projection, cotangent[0]
    )
    encoded, attended, gradient = publish(*results)
    return encoded[None], attended[None], gradient


def solution(mesh):
    in_specs = (
        P("rep", "space", None),
        P("rep", "space", None),
        P("rep", "space"),
        P(),
        P(),
        P(),
        P("rep", "space", None),
    )
    out_specs = (P("rep", "space", None), P("rep", "space", None), P())
    return jax.shard_map(local, mesh=mesh, in_specs=in_specs, out_specs=out_specs, check_vma=False)
```

```python
import functools
import math

import jax
import jax.numpy as jnp
from jax import lax
from jax.experimental import pallas as pl
from jax.experimental.pallas import tpu as pltpu
from jax.sharding import PartitionSpec as P

HEADS = 16
EDGE = 8
MESH = pl.DeviceIdType.MESH
F32 = jnp.float32
BF16 = jnp.bfloat16
VMEM_LIMIT = 60 * 1024 * 1024


def dot(a, b):
    return jnp.dot(a, b, preferred_element_type=F32)


def dot_t(a, b):
    return lax.dot_general(a, b, (((1,), (1,)), ((), ())), preferred_element_type=F32)


def iota(shape, dim):
    return lax.broadcasted_iota(jnp.int32, shape, dim)


def onehot(mask):
    return jnp.where(mask, 1.0, 0.0).astype(BF16)


def front_body(
    spaces, reps, cap, feat, nb, order, w_hbm, enc_out, enc, reg, enc_sem, loads, meanwhile,
    w, x, halo_l, halo_r, table, passed, got, send, recv, place, picks, held,
    w_sem, hs, hr, ts, tr, us, ur, rs, rr,
):
    me = lax.axis_index("space")
    rows, width = feat.shape
    face = EDGE * EDGE
    brick = EDGE * face
    bricks = rows // brick
    outer, inner = got.shape[:2]
    line, within = me // inner, lax.rem(me, inner)
    load = pltpu.make_async_copy(w_hbm, w, w_sem)
    load.start()
    for later in loads:
        later.start()

    def peer(k):
        return {"space": lax.rem(me + k, spaces)}

    barrier = pltpu.get_barrier_semaphore()

    def greet(k, carry):
        pl.semaphore_signal(barrier, inc=1, device_id=peer(k), device_id_type=MESH)
        return carry

    lax.fori_loop(1, spaces, greet, 0)
    rep = lax.axis_index("rep")
    for m in range(1, reps):
        for core in range(2):
            device = {"space": me // 2 * 2 + core, "rep": lax.rem(rep + m, reps)}
            pl.semaphore_signal(barrier, inc=1, device_id=device, device_id_type=MESH)

    depth = iota((EDGE + 2, EDGE, width), 1)

    def beside(b, offset, source_id):
        p, q, r = offset
        number = 9 * (p + 1) + 3 * (q + 1) + (r + 1)
        number -= number > 13
        target = nb[b, number]
        return jnp.where((target == source_id) & (target >= 0), 1.0, 0.0)

    def layer(ref, first):
        return ref[pl.ds(first, face)].astype(F32).reshape(EDGE, EDGE, width)

    def write_layer(b, i, p, sources, ids, own):
        grown = []
        for r in (-1, 0, 1):
            parts = []
            for q in (-1, 0, 1):
                part = slice(EDGE - 1, EDGE) if q < 0 else slice(0, 1) if q > 0 else slice(0, EDGE)
                if own is not None and q == 0 and r == 0:
                    parts.append(own)
                    continue
                total = None
                for source, one_id in zip(sources, ids):
                    term = source[part] * beside(b, (p, q, r), one_id)
                    total = term if total is None else total + term
                parts.append(total)
            grown.append(jnp.concatenate(parts, axis=0))
        below, here, above = grown
        variants = (
            pltpu.roll(jnp.where(depth == EDGE - 1, below, here), 1, 1),
            here,
            pltpu.roll(jnp.where(depth == 0, above, here), EDGE - 1, 1),
        )
        first = (i * bricks + b) * face
        first = first if isinstance(first, int) else pl.multiple_of(first, face)
        for q in range(3):
            for r in range(3):
                n = 3 * q + r
                x[pl.ds(first, face), n * width : (n + 1) * width] = (
                    variants[r][q : q + EDGE].reshape(face, width).astype(BF16)
                )

    own_ids = [me * bricks + n for n in range(bricks)]
    left_ids = [(me - 1) * bricks + n for n in range(bricks)]
    right_ids = [(me + 1) * bricks + n for n in range(bricks)]

    def inner_layer(i, carry):
        sources = [layer(feat, pl.multiple_of(n * brick + i * face, face)) for n in range(bricks)]
        for b in range(bricks):
            write_layer(b, i + 1, 0, sources, own_ids, sources[b])
        return carry

    lax.fori_loop(0, EDGE, inner_layer, 0)

    places = order[...]
    shift = rows.bit_length() - 1
    owner = lax.shift_right_logical(places, shift)
    slot = places & (rows - 1)
    ahead = (owner - me + spaces) & (spaces - 1)
    chosen = jnp.where(iota((spaces, rows), 0) == owner, 1.0, 0.0)
    before = onehot(iota((rows, rows), 0) < iota((rows, rows), 1))
    rank = jnp.sum(chosen * dot(chosen.astype(BF16), before), axis=0, keepdims=True)
    high = lax.shift_right_logical(slot, 5).astype(F32)
    low = (slot & 31).astype(F32)
    lanes = table.shape[3]
    by_rank = onehot(iota((lanes, rows), 0).astype(F32) == rank)
    stacked = jnp.concatenate([chosen * high, chosen * low, chosen], axis=0).astype(BF16)
    found = dot_t(stacked, by_rank)
    slots = found[:spaces] * 32.0 + found[spaces : 2 * spaces]
    slots = jnp.where(found[2 * spaces :] > 0.5, slots, -1.0)
    for n in range(outer):
        table[:, n] = jnp.broadcast_to(slots[n * inner : (n + 1) * inner][:, None, :], (inner, 8, lanes))
    row_at = ahead.astype(F32) * float(cap) + rank

    pl.semaphore_wait(barrier, spaces - 1 + 2 * (reps - 1))

    halos = []
    for b in range(bricks):
        for source, dst, step, n in (
            (b * brick + brick - face, halo_l, 1, 2 * b),
            (b * brick, halo_r, spaces - 1, 2 * b + 1),
        ):
            copy = pltpu.make_async_remote_copy(
                src_ref=feat.at[pl.ds(source, face)], dst_ref=dst.at[b], send_sem=hs.at[n], recv_sem=hr.at[n],
                device_id=peer(step), device_id_type=MESH,
            )
            copy.start()
            halos.append(copy)

    def inner_table(n, sender):
        return pltpu.make_async_remote_copy(
            src_ref=table.at[lax.rem(within + n, inner)], dst_ref=passed.at[sender], send_sem=ts.at[n], recv_sem=tr.at[n],
            device_id={"space": line * inner + lax.rem(within + n, inner)}, device_id_type=MESH,
        )

    def outer_table(n, sender):
        there = lax.rem(line + n, outer)
        return pltpu.make_async_remote_copy(
            src_ref=passed.at[:, there], dst_ref=got.at[sender], send_sem=us.at[n], recv_sem=ur.at[n],
            device_id={"space": there * inner + within}, device_id_type=MESH,
        )

    def row_copy(k):
        return pltpu.make_async_remote_copy(
            src_ref=send.at[k], dst_ref=recv.at[k], send_sem=rs.at[k], recv_sem=rr.at[k],
            device_id=peer(k), device_id_type=MESH,
        )

    for n in range(1, inner):
        inner_table(n, within).start()

    load.wait()
    halves = EDGE // 2
    block = halves * bricks * face
    group = 8

    def product(n, p):
        first = pl.multiple_of((n * halves + p) * bricks * face, face)
        return dot(x[pl.ds(first, block), :], w[pl.ds(9 * p, 9)].reshape(9 * width, width))

    def conv_first(n, carry):
        held[n] = product(n, 1) + product(n, 2 - 2 * n)
        part = spaces * cap // 2
        wanted = (iota((part, rows), 0) + n * part).astype(F32)
        picks[pl.ds(pl.multiple_of(n * part, 128), part)] = onehot(wanted == row_at)
        return carry

    lax.fori_loop(0, 2, conv_first, 0)
    passed[within] = table[within]
    for n in range(1, inner):
        inner_table(n, within).wait_send()
        inner_table(n, lax.rem(within - n + inner, inner)).wait_recv()
    for n in range(1, outer):
        outer_table(n, line).start()
    for copy in halos:
        copy.wait_recv()
    tops = [layer(feat, n * brick + brick - face) for n in range(bricks)]
    bottoms = [layer(feat, n * brick) for n in range(bricks)]
    lefts = [layer(halo_l.at[n], 0) for n in range(bricks)]
    rights = [layer(halo_r.at[n], 0) for n in range(bricks)]
    for b in range(bricks):
        write_layer(b, 0, -1, lefts + tops, left_ids + own_ids, None)
        write_layer(b, EDGE + 1, 1, bottoms + rights, own_ids + right_ids, None)

    def conv_last(n, carry):
        total = held[n] + product(n, 2 * n)
        for i in range(halves):
            for b in range(bricks):
                at = pl.ds(pl.multiple_of(b * brick + (n * halves + i) * face, face), face)
                rows_in = (i * bricks + b) * face
                enc[at] = (feat[at].astype(F32) + total[rows_in : rows_in + face]).astype(BF16)
        return carry

    lax.fori_loop(0, 2, conv_last, 0)
    pltpu.make_async_copy(enc, enc_out, enc_sem).start()

    for c in range(spaces // group):
        block = dot(picks[c * group * cap : (c + 1) * group * cap], enc[...]).astype(BF16)
        send[c * group : (c + 1) * group] = block.reshape(group, cap, width)
        for k in range(max(1, c * group), (c + 1) * group):
            row_copy(k).start()
    recv[0] = send[0]
    meanwhile()
    for n in range(inner):
        got[line, n] = passed[n, line]
    for n in range(1, outer):
        outer_table(n, line).wait_send()
        outer_table(n, lax.rem(line - n + outer, outer)).wait_recv()
    column = iota((8, 128), 1)
    for t in range(spaces * cap // 128):
        lane = jnp.full((8, 128), -1.0, F32)
        for k in range(spaces):
            start, end = max(0, k * cap - 128 * t), min(128, (k + 1) * cap - 128 * t)
            if start >= end:
                continue
            source = lax.rem(me - k + spaces, spaces)
            moved = got[source // inner, lax.rem(source, inner)]
            if (k * cap - 128 * t) % 128:
                moved = pltpu.roll(moved, (k * cap - 128 * t) % 128, 1)
            lane = jnp.where((column >= start) & (column < end), moved, lane)
        place[:, t * 128 : (t + 1) * 128] = onehot(iota((rows, 128), 0).astype(F32) == lane[0:1])
    total = jnp.zeros((rows, width), F32)
    for c in range(spaces // group):
        for k in range(max(1, c * group), (c + 1) * group):
            row_copy(k).wait_recv()
        arrived = recv[c * group : (c + 1) * group].reshape(group * cap, width)
        total = total + dot(place[:, c * group * cap : (c + 1) * group * cap], arrived)
    reg[...] = total.astype(BF16)

    def wait_sent(k, carry):
        row_copy(k).wait_send()
        return carry

    lax.fori_loop(1, spaces, wait_sent, 0)
    for copy in halos:
        copy.wait_send()


def attention_body(
    spaces, reps, reg, wi, wo, cot, att_out, att, grad_out, grad, loads, att_sem, grad_sems,
    q, k, v, ctx, s0, s1, *comm,
):
    chunks = [comm[n : n + 11] for n in range(0, len(comm), 11)]
    rows, width = reg.shape
    head = width // HEADS
    half = width // 2
    space, rep = lax.axis_index("space"), lax.axis_index("rep")
    planes, others = spaces // 2, 2 * reps
    chip, core = space // 2, space % 2
    place = rep * 2 + core

    side = math.isqrt(planes)
    far_first = sorted(range(1, planes), key=lambda n: -sum(min(d, side - d) for d in (n // side, n % side)))

    def across(n):
        return {"space": lax.rem(chip + n, planes) * 2 + core}

    def along(n):
        there = lax.rem(place + n, others)
        return {"space": chip * 2 + there % 2, "rep": there // 2}

    def run(count, make):
        def body(n, carry):
            make(n)
            return carry

        lax.fori_loop(1, count, body, 0)

    def copy(src, dst, send, recv, device):
        return pltpu.make_async_remote_copy(
            src_ref=src, dst_ref=dst, send_sem=send, recv_sem=recv, device_id=device, device_id_type=MESH
        )

    def scatter(c, n):
        term, first, part, second, final, s1, r1, s2, r2, s3, r3 = chunks[c]
        return copy(term.at[lax.rem(place + n, others)], first.at[n], s1.at[n], r1.at[n], along(n))

    def share(c, n, sender):
        term, first, part, second, final, s1, r1, s2, r2, s3, r3 = chunks[c]
        return copy(part, second.at[sender], s2.at[n], r2.at[n], across(n))

    def gather(c, n, sender):
        term, first, part, second, final, s1, r1, s2, r2, s3, r3 = chunks[c]
        return copy(final.at[sender], final.at[sender], s3.at[n], r3.at[n], along(n))

    def start_scatter(c, values):
        chunks[c][0][...] = values.reshape(chunks[c][0].shape)
        run(others, lambda n: scatter(c, n).start())

    def start_share(c):
        term, first, part, second = chunks[c][:4]
        first[0] = term[place]
        run(others, lambda n: scatter(c, n).wait())
        part[...] = jnp.sum(first[...], axis=0)
        for n in far_first:
            share(c, n, chip).start()

    def start_gather(c):
        part, second, final = chunks[c][2:5]
        second[chip] = part[...]
        run(planes, lambda n: share(c, n, chip).wait_send())
        run(planes, lambda n: share(c, n, lax.rem(chip - n + planes, planes)).wait_recv())
        final[place] = jnp.sum(second[...], axis=0)
        run(others, lambda n: gather(c, n, place).start())

    def finish(c, at):
        final = chunks[c][4]
        run(others, lambda n: gather(c, n, place).wait_send())
        run(others, lambda n: gather(c, n, lax.rem(place - n + others, others)).wait_recv())
        grad[at] = final[...].reshape(-1, width)
        pltpu.make_async_copy(grad.at[at], grad_out.at[at], grad_sems.at[c]).start()

    def gradient_rows(side):
        part_context = ctx[side].astype(BF16)
        return lax.dot_general(part_context, cot[...], (((0,), (0,)), ((), ())), preferred_element_type=F32)

    for load in loads:
        load.wait()
    residual = reg[...].astype(F32)
    centred = residual - jnp.mean(residual, axis=-1, keepdims=True)
    variance = jnp.mean(centred * centred, axis=-1, keepdims=True)
    normed = (centred * lax.rsqrt(variance + 1e-05)).astype(BF16)
    packed = dot(normed, wi[...]).astype(BF16)
    q[...] = packed[:, :width] * jnp.asarray(head**-0.5, BF16)
    k[...] = packed[:, width : 2 * width]
    for n in range(2):
        v[n, :, :half] = packed[:, 2 * width + n * half : 2 * width + (n + 1) * half]
    tile = s0.shape[0]
    tiles = rows // tile
    lane_q = iota((tile, width), 1) // head
    lane_c = iota((tile, half), 1) // head
    held = (s0, s1)

    def scores(h, t):
        queries = jnp.where(lane_q == h, q[t * tile : (t + 1) * tile], jnp.zeros((), BF16))
        return dot_t(queries, k[...])

    def one_head(h):
        side = h // (HEADS // 2)
        for t in range(tiles):
            later = h if t < tiles - 1 else jnp.minimum(h + 1, HEADS - 1)
            held[(t + 1) % 2][...] = scores(later, (t + 1) % tiles)
            now = held[t % 2][...]
            lifted = jnp.exp(now - jnp.max(now, axis=-1, keepdims=True))
            both = dot(lifted.astype(BF16), v[side])
            at = slice(t * tile, (t + 1) * tile)
            ctx[side, at] += jnp.where(lane_c == h - side * (HEADS // 2), both[:, :half] / both[:, half:], 0.0)

    s0[...] = scores(0, 0)
    heads_a_step = HEADS // 4

    def step(n, carry):
        for m in range(heads_a_step):
            one_head(heads_a_step * n + m)

        @pl.when(n == 1)
        def _():
            start_scatter(0, gradient_rows(0))

        @pl.when(n == 2)
        def _():
            start_scatter(1, gradient_rows(1)[: half // 2])
            start_share(0)

        return carry

    lax.fori_loop(0, 4, step, 0)
    start_scatter(2, gradient_rows(1)[half // 2 :])
    start_share(1)
    context = jnp.concatenate([ctx[0], ctx[1]], axis=1).astype(BF16)
    att[...] = (reg[...].astype(F32) + dot(context, wo[...])).astype(BF16)
    pltpu.make_async_copy(att, att_out, att_sem).start()
    start_share(2)
    start_gather(0)
    start_gather(1)
    finish(0, pl.ds(0, half))
    start_gather(2)
    finish(1, pl.ds(half, half // 2))
    finish(2, pl.ds(half + half // 2, half // 2))
    for c, at in enumerate((pl.ds(0, half), pl.ds(half, half // 2), pl.ds(half + half // 2, half // 2))):
        pltpu.make_async_copy(grad.at[at], grad_out.at[at], grad_sems.at[c]).wait()


def layer_kernel(spaces, reps, cap, feat, nb, order, *refs):
    w_hbm, wi_hbm, wo_hbm, cot_hbm, enc_out, att_out, grad_out = refs[:7]
    wi, wo, cot, enc, reg, att, grad, sems = refs[7:15]
    front_refs, attention_refs = refs[15:36], refs[36:]
    v, ctx = attention_refs[3:5]
    loads = [
        pltpu.make_async_copy(source, held, sems.at[n])
        for n, (source, held) in enumerate(((wi_hbm, wi), (wo_hbm, wo), (cot_hbm, cot)))
    ]

    def meanwhile():
        v[:, :, ctx.shape[2] :] = jnp.ones(ctx.shape, BF16)
        ctx[...] = jnp.zeros_like(ctx)

    front_body(spaces, reps, cap, feat, nb, order, w_hbm, enc_out, enc, reg, sems.at[3], loads, meanwhile, *front_refs)
    grad_sems = attention_refs[0]
    attention_body(
        spaces, reps, reg, wi, wo, cot, att_out, att, grad_out, grad, loads, sems.at[4], grad_sems, *attention_refs[1:]
    )
    pltpu.make_async_copy(enc, enc_out, sems.at[3]).wait()
    pltpu.make_async_copy(att, att_out, sems.at[4]).wait()


def layer(features, neighbours, order, weight, wi, wo, cot):
    spaces, reps = lax.axis_size("space"), lax.axis_size("rep")
    rows, width = features.shape
    cap = 3 * rows // (2 * spaces)
    bricks = rows // EDGE**3
    face = EDGE * EDGE
    half = width // 2
    inner, outer = 8, spaces // 8
    planes, others = spaces // 2, 2 * reps
    tile = 256
    vmem = pl.BlockSpec(memory_space=pltpu.VMEM)
    hbm = pl.BlockSpec(memory_space=pl.ANY)
    dma = pltpu.SemaphoreType.DMA
    full = pltpu.VMEM((rows, width), BF16)
    shared = [
        pltpu.VMEM(wi.shape, BF16),
        pltpu.VMEM(wo.shape, BF16),
        *[full] * 4,
        pltpu.VMEM((width, width), F32),
        dma((5,)),
    ]
    for_front = [
        pltpu.VMEM(weight.shape, BF16),
        pltpu.VMEM(((EDGE + 2) * bricks * face, 9 * width), BF16),
        pltpu.VMEM((bricks, face, width), BF16),
        pltpu.VMEM((bricks, face, width), BF16),
        pltpu.VMEM((inner, outer, 8, 128), F32),
        pltpu.VMEM((inner, outer, 8, 128), F32),
        pltpu.VMEM((outer, inner, 8, 128), F32),
        pltpu.VMEM((spaces, cap, width), BF16),
        pltpu.VMEM((spaces, cap, width), BF16),
        pltpu.VMEM((rows, spaces * cap), BF16),
        pltpu.VMEM((spaces * cap, rows), BF16),
        pltpu.VMEM((2, rows // 2, width), F32),
        dma,
        dma((2 * bricks,)),
        dma((2 * bricks,)),
        *[dma((inner,))] * 2,
        *[dma((outer,))] * 2,
        *[dma((spaces,))] * 2,
    ]
    for_attention = [
        dma((3,)),
        full,
        full,
        pltpu.VMEM((2, rows, width), BF16),
        pltpu.VMEM((2, rows, half), F32),
        pltpu.VMEM((tile, rows), F32),
        pltpu.VMEM((tile, rows), F32),
    ]
    for count in (half, half // 2, half // 2):
        for_attention += [
            pltpu.VMEM((others, count // others, width), F32),
            pltpu.VMEM((others, count // others, width), F32),
            pltpu.VMEM((count // others, width), F32),
            pltpu.VMEM((planes, count // others, width), F32),
            pltpu.VMEM((others, count // others, width), F32),
            *[dma((others,))] * 2,
            *[dma((planes,))] * 2,
            *[dma((others,))] * 2,
        ]
    return pl.pallas_call(
        functools.partial(layer_kernel, spaces, reps, cap),
        out_shape=[
            jax.ShapeDtypeStruct((rows, width), BF16),
            jax.ShapeDtypeStruct((rows, width), BF16),
            jax.ShapeDtypeStruct((width, width), F32),
        ],
        in_specs=[vmem, pl.BlockSpec(memory_space=pltpu.SMEM), vmem, hbm, hbm, hbm, hbm],
        out_specs=[hbm] * 3,
        scratch_shapes=shared + for_front + for_attention,
        compiler_params=pltpu.CompilerParams(collective_id=0, has_side_effects=True, vmem_limit_bytes=VMEM_LIMIT),
        cost_estimate=pl.CostEstimate(
            flops=2 * rows * 27 * width * width + 4 * HEADS * rows * rows * width,
            bytes_accessed=weight.size * 2 + 12 * rows * width,
            transcendentals=HEADS * rows * rows,
        ),
        name="layer",
    )(features, neighbours, order, weight, wi, wo, cot)


def publish_kernel(count, *refs):
    given, made, held, sems = refs[:count], refs[count : 2 * count], refs[2 * count : 3 * count], refs[3 * count]
    reads = [pltpu.make_async_copy(given[n], held[n], sems.at[0, n]) for n in range(count)]
    writes = [pltpu.make_async_copy(held[n], made[n], sems.at[1, n]) for n in range(count)]
    for read in reads:
        read.start()
    for read, write in zip(reads, writes):
        read.wait()
        write.start()
    for write in writes:
        write.wait()


def publish(*arrays):
    spec = pl.BlockSpec(memory_space=pl.ANY)
    return pl.pallas_call(
        functools.partial(publish_kernel, len(arrays)),
        out_shape=[jax.ShapeDtypeStruct(a.shape, a.dtype) for a in arrays],
        in_specs=[spec] * len(arrays),
        out_specs=[spec] * len(arrays),
        scratch_shapes=[pltpu.VMEM(a.shape, a.dtype) for a in arrays] + [pltpu.SemaphoreType.DMA((2, len(arrays)))],
        name="publish",
    )(*arrays)


def local(features, neighbours, serial_order, kernel_weight, input_projection, output_projection, cotangent):
    results = layer(
        features[0], neighbours[0], serial_order, kernel_weight, input_projection, output_projection, cotangent[0]
    )
    encoded, attended, gradient = publish(*results)
    return encoded[None], attended[None], gradient


def solution(mesh):
    in_specs = (
        P("rep", "space", None),
        P("rep", "space", None),
        P("rep", "space"),
        P(),
        P(),
        P(),
        P("rep", "space", None),
    )
    out_specs = (P("rep", "space", None), P("rep", "space", None), P())
    return jax.shard_map(local, mesh=mesh, in_specs=in_specs, out_specs=out_specs, check_vma=False)
```

```python
import functools
import math

import jax
import jax.numpy as jnp
from jax import lax
from jax.experimental import pallas as pl
from jax.experimental.pallas import tpu as pltpu
from jax.sharding import PartitionSpec as P

HEADS = 16
EDGE = 8
MESH = pl.DeviceIdType.MESH
F32 = jnp.float32
BF16 = jnp.bfloat16
VMEM_LIMIT = 60 * 1024 * 1024


def dot(a, b):
    return jnp.dot(a, b, preferred_element_type=F32)


def dot_t(a, b):
    return lax.dot_general(a, b, (((1,), (1,)), ((), ())), preferred_element_type=F32)


def iota(shape, dim):
    return lax.broadcasted_iota(jnp.int32, shape, dim)


def onehot(mask):
    return jnp.where(mask, 1.0, 0.0).astype(BF16)


def front_body(
    spaces, reps, cap, feat, nb, order, w_hbm, enc_out, enc, reg, enc_sem, loads, meanwhile,
    w, x, halo_l, halo_r, table, passed, got, send, recv, place, picks, held,
    w_sem, hs, hr, ts, tr, us, ur, rs, rr,
):
    me = lax.axis_index("space")
    rows, width = feat.shape
    face = EDGE * EDGE
    brick = EDGE * face
    bricks = rows // brick
    outer, inner = got.shape[:2]
    line, within = me // inner, lax.rem(me, inner)
    load = pltpu.make_async_copy(w_hbm, w, w_sem)
    load.start()
    for later in loads:
        later.start()

    def peer(k):
        return {"space": lax.rem(me + k, spaces)}

    barrier = pltpu.get_barrier_semaphore()

    def greet(k, carry):
        pl.semaphore_signal(barrier, inc=1, device_id=peer(k), device_id_type=MESH)
        return carry

    lax.fori_loop(1, spaces, greet, 0)
    rep = lax.axis_index("rep")
    for m in range(1, reps):
        for core in range(2):
            device = {"space": me // 2 * 2 + core, "rep": lax.rem(rep + m, reps)}
            pl.semaphore_signal(barrier, inc=1, device_id=device, device_id_type=MESH)

    depth = iota((EDGE + 2, EDGE, width), 1)

    def beside(b, offset, source_id):
        p, q, r = offset
        number = 9 * (p + 1) + 3 * (q + 1) + (r + 1)
        number -= number > 13
        target = nb[b, number]
        return jnp.where((target == source_id) & (target >= 0), 1.0, 0.0)

    def layer(ref, first):
        return ref[pl.ds(first, face)].astype(F32).reshape(EDGE, EDGE, width)

    def write_layer(b, i, p, sources, ids, own):
        grown = []
        for r in (-1, 0, 1):
            parts = []
            for q in (-1, 0, 1):
                part = slice(EDGE - 1, EDGE) if q < 0 else slice(0, 1) if q > 0 else slice(0, EDGE)
                if own is not None and q == 0 and r == 0:
                    parts.append(own)
                    continue
                total = None
                for source, one_id in zip(sources, ids):
                    term = source[part] * beside(b, (p, q, r), one_id)
                    total = term if total is None else total + term
                parts.append(total)
            grown.append(jnp.concatenate(parts, axis=0))
        below, here, above = grown
        variants = (
            pltpu.roll(jnp.where(depth == EDGE - 1, below, here), 1, 1),
            here,
            pltpu.roll(jnp.where(depth == 0, above, here), EDGE - 1, 1),
        )
        first = (i * bricks + b) * face
        first = first if isinstance(first, int) else pl.multiple_of(first, face)
        for q in range(3):
            for r in range(3):
                n = 3 * q + r
                x[pl.ds(first, face), n * width : (n + 1) * width] = (
                    variants[r][q : q + EDGE].reshape(face, width).astype(BF16)
                )

    own_ids = [me * bricks + n for n in range(bricks)]
    left_ids = [(me - 1) * bricks + n for n in range(bricks)]
    right_ids = [(me + 1) * bricks + n for n in range(bricks)]

    def inner_layer(i, carry):
        sources = [layer(feat, pl.multiple_of(n * brick + i * face, face)) for n in range(bricks)]
        for b in range(bricks):
            write_layer(b, i + 1, 0, sources, own_ids, sources[b])
        return carry

    lax.fori_loop(0, EDGE, inner_layer, 0)

    places = order[...]
    shift = rows.bit_length() - 1
    owner = lax.shift_right_logical(places, shift)
    slot = places & (rows - 1)
    ahead = (owner - me + spaces) & (spaces - 1)
    chosen = jnp.where(iota((spaces, rows), 0) == owner, 1.0, 0.0)
    before = onehot(iota((rows, rows), 0) < iota((rows, rows), 1))
    rank = jnp.sum(chosen * dot(chosen.astype(BF16), before), axis=0, keepdims=True)
    high = lax.shift_right_logical(slot, 5).astype(F32)
    low = (slot & 31).astype(F32)
    lanes = table.shape[3]
    by_rank = onehot(iota((lanes, rows), 0).astype(F32) == rank)
    stacked = jnp.concatenate([chosen * high, chosen * low, chosen], axis=0).astype(BF16)
    found = dot_t(stacked, by_rank)
    slots = found[:spaces] * 32.0 + found[spaces : 2 * spaces]
    slots = jnp.where(found[2 * spaces :] > 0.5, slots, -1.0)
    for n in range(outer):
        table[:, n] = jnp.broadcast_to(slots[n * inner : (n + 1) * inner][:, None, :], (inner, 8, lanes))
    row_at = ahead.astype(F32) * float(cap) + rank

    pl.semaphore_wait(barrier, spaces - 1 + 2 * (reps - 1))

    halos = []
    for b in range(bricks):
        for source, dst, step, n in (
            (b * brick + brick - face, halo_l, 1, 2 * b),
            (b * brick, halo_r, spaces - 1, 2 * b + 1),
        ):
            copy = pltpu.make_async_remote_copy(
                src_ref=feat.at[pl.ds(source, face)], dst_ref=dst.at[b], send_sem=hs.at[n], recv_sem=hr.at[n],
                device_id=peer(step), device_id_type=MESH,
            )
            copy.start()
            halos.append(copy)

    def inner_table(n, sender):
        return pltpu.make_async_remote_copy(
            src_ref=table.at[lax.rem(within + n, inner)], dst_ref=passed.at[sender], send_sem=ts.at[n], recv_sem=tr.at[n],
            device_id={"space": line * inner + lax.rem(within + n, inner)}, device_id_type=MESH,
        )

    def outer_table(n, sender):
        there = lax.rem(line + n, outer)
        return pltpu.make_async_remote_copy(
            src_ref=passed.at[:, there], dst_ref=got.at[sender], send_sem=us.at[n], recv_sem=ur.at[n],
            device_id={"space": there * inner + within}, device_id_type=MESH,
        )

    def row_copy(k):
        return pltpu.make_async_remote_copy(
            src_ref=send.at[k], dst_ref=recv.at[k], send_sem=rs.at[k], recv_sem=rr.at[k],
            device_id=peer(k), device_id_type=MESH,
        )

    for n in range(1, inner):
        inner_table(n, within).start()

    load.wait()
    halves = EDGE // 2
    block = halves * bricks * face
    group = 8

    def product(n, p):
        first = pl.multiple_of((n * halves + p) * bricks * face, face)
        return dot(x[pl.ds(first, block), :], w[pl.ds(9 * p, 9)].reshape(9 * width, width))

    def conv_first(n, carry):
        held[n] = product(n, 1) + product(n, 2 - 2 * n)
        part = spaces * cap // 2
        wanted = (iota((part, rows), 0) + n * part).astype(F32)
        picks[pl.ds(pl.multiple_of(n * part, 128), part)] = onehot(wanted == row_at)
        return carry

    lax.fori_loop(0, 2, conv_first, 0)
    passed[within] = table[within]
    for n in range(1, inner):
        inner_table(n, within).wait_send()
        inner_table(n, lax.rem(within - n + inner, inner)).wait_recv()
    for n in range(1, outer):
        outer_table(n, line).start()
    for copy in halos:
        copy.wait_recv()
    tops = [layer(feat, n * brick + brick - face) for n in range(bricks)]
    bottoms = [layer(feat, n * brick) for n in range(bricks)]
    lefts = [layer(halo_l.at[n], 0) for n in range(bricks)]
    rights = [layer(halo_r.at[n], 0) for n in range(bricks)]
    for b in range(bricks):
        write_layer(b, 0, -1, lefts + tops, left_ids + own_ids, None)
        write_layer(b, EDGE + 1, 1, bottoms + rights, own_ids + right_ids, None)

    def conv_last(n, carry):
        total = held[n] + product(n, 2 * n)
        for i in range(halves):
            for b in range(bricks):
                at = pl.ds(pl.multiple_of(b * brick + (n * halves + i) * face, face), face)
                rows_in = (i * bricks + b) * face
                enc[at] = (feat[at].astype(F32) + total[rows_in : rows_in + face]).astype(BF16)
        return carry

    lax.fori_loop(0, 2, conv_last, 0)
    pltpu.make_async_copy(enc, enc_out, enc_sem).start()

    lines = spaces // group
    order_of_lines = sorted(range(lines), key=lambda c: -min(c, lines - c))
    for c in order_of_lines:
        block = dot(picks[c * group * cap : (c + 1) * group * cap], enc[...]).astype(BF16)
        send[c * group : (c + 1) * group] = block.reshape(group, cap, width)
        for k in range(max(1, c * group), (c + 1) * group):
            row_copy(k).start()
    recv[0] = send[0]
    meanwhile()
    for n in range(inner):
        got[line, n] = passed[n, line]
    for n in range(1, outer):
        outer_table(n, line).wait_send()
        outer_table(n, lax.rem(line - n + outer, outer)).wait_recv()
    column = iota((8, 128), 1)
    for t in range(spaces * cap // 128):
        lane = jnp.full((8, 128), -1.0, F32)
        for k in range(spaces):
            start, end = max(0, k * cap - 128 * t), min(128, (k + 1) * cap - 128 * t)
            if start >= end:
                continue
            source = lax.rem(me - k + spaces, spaces)
            moved = got[source // inner, lax.rem(source, inner)]
            if (k * cap - 128 * t) % 128:
                moved = pltpu.roll(moved, (k * cap - 128 * t) % 128, 1)
            lane = jnp.where((column >= start) & (column < end), moved, lane)
        place[:, t * 128 : (t + 1) * 128] = onehot(iota((rows, 128), 0).astype(F32) == lane[0:1])
    total = jnp.zeros((rows, width), F32)
    for c in order_of_lines:
        for k in range(max(1, c * group), (c + 1) * group):
            row_copy(k).wait_recv()
        arrived = recv[c * group : (c + 1) * group].reshape(group * cap, width)
        total = total + dot(place[:, c * group * cap : (c + 1) * group * cap], arrived)
    reg[...] = total.astype(BF16)

    def wait_sent(k, carry):
        row_copy(k).wait_send()
        return carry

    lax.fori_loop(1, spaces, wait_sent, 0)
    for copy in halos:
        copy.wait_send()


def attention_body(
    spaces, reps, reg, wi, wo, cot, att_out, att, grad_out, grad, loads, att_sem, grad_sems,
    q, k, v, ctx, s0, s1, *comm,
):
    chunks = [comm[n : n + 11] for n in range(0, len(comm), 11)]
    rows, width = reg.shape
    head = width // HEADS
    half = width // 2
    space, rep = lax.axis_index("space"), lax.axis_index("rep")
    planes, others = spaces // 2, 2 * reps
    chip, core = space // 2, space % 2
    place = rep * 2 + core

    side = math.isqrt(planes)
    far_first = sorted(range(1, planes), key=lambda n: -sum(min(d, side - d) for d in (n // side, n % side)))

    def across(n):
        return {"space": lax.rem(chip + n, planes) * 2 + core}

    def along(n):
        there = lax.rem(place + n, others)
        return {"space": chip * 2 + there % 2, "rep": there // 2}

    def run(count, make):
        def body(n, carry):
            make(n)
            return carry

        lax.fori_loop(1, count, body, 0)

    def copy(src, dst, send, recv, device):
        return pltpu.make_async_remote_copy(
            src_ref=src, dst_ref=dst, send_sem=send, recv_sem=recv, device_id=device, device_id_type=MESH
        )

    def scatter(c, n):
        term, first, part, second, final, s1, r1, s2, r2, s3, r3 = chunks[c]
        return copy(term.at[lax.rem(place + n, others)], first.at[n], s1.at[n], r1.at[n], along(n))

    def share(c, n, sender):
        term, first, part, second, final, s1, r1, s2, r2, s3, r3 = chunks[c]
        return copy(part, second.at[sender], s2.at[n], r2.at[n], across(n))

    def gather(c, n, sender):
        term, first, part, second, final, s1, r1, s2, r2, s3, r3 = chunks[c]
        return copy(final.at[sender], final.at[sender], s3.at[n], r3.at[n], along(n))

    def start_scatter(c, values):
        chunks[c][0][...] = values.reshape(chunks[c][0].shape)
        run(others, lambda n: scatter(c, n).start())

    def start_share(c):
        term, first, part, second = chunks[c][:4]
        first[0] = term[place]
        run(others, lambda n: scatter(c, n).wait())
        part[...] = jnp.sum(first[...], axis=0)
        for n in far_first:
            share(c, n, chip).start()

    def start_gather(c):
        part, second, final = chunks[c][2:5]
        second[chip] = part[...]
        run(planes, lambda n: share(c, n, chip).wait_send())
        run(planes, lambda n: share(c, n, lax.rem(chip - n + planes, planes)).wait_recv())
        final[place] = jnp.sum(second[...], axis=0)
        run(others, lambda n: gather(c, n, place).start())

    def finish(c, at):
        final = chunks[c][4]
        run(others, lambda n: gather(c, n, place).wait_send())
        run(others, lambda n: gather(c, n, lax.rem(place - n + others, others)).wait_recv())
        grad[at] = final[...].reshape(-1, width)
        pltpu.make_async_copy(grad.at[at], grad_out.at[at], grad_sems.at[c]).start()

    def gradient_rows(side):
        part_context = ctx[side].astype(BF16)
        return lax.dot_general(part_context, cot[...], (((0,), (0,)), ((), ())), preferred_element_type=F32)

    for load in loads:
        load.wait()
    residual = reg[...].astype(F32)
    centred = residual - jnp.mean(residual, axis=-1, keepdims=True)
    variance = jnp.mean(centred * centred, axis=-1, keepdims=True)
    normed = (centred * lax.rsqrt(variance + 1e-05)).astype(BF16)
    packed = dot(normed, wi[...]).astype(BF16)
    q[...] = packed[:, :width] * jnp.asarray(head**-0.5, BF16)
    k[...] = packed[:, width : 2 * width]
    for n in range(2):
        v[n, :, :half] = packed[:, 2 * width + n * half : 2 * width + (n + 1) * half]
    tile = s0.shape[0]
    tiles = rows // tile
    lane_q = iota((tile, width), 1) // head
    lane_c = iota((tile, half), 1) // head
    held = (s0, s1)

    def scores(h, t):
        queries = jnp.where(lane_q == h, q[t * tile : (t + 1) * tile], jnp.zeros((), BF16))
        return dot_t(queries, k[...])

    def one_head(h):
        side = h // (HEADS // 2)
        for t in range(tiles):
            later = h if t < tiles - 1 else jnp.minimum(h + 1, HEADS - 1)
            held[(t + 1) % 2][...] = scores(later, (t + 1) % tiles)
            now = held[t % 2][...]
            lifted = jnp.exp(now - jnp.max(now, axis=-1, keepdims=True))
            both = dot(lifted.astype(BF16), v[side])
            at = slice(t * tile, (t + 1) * tile)
            ctx[side, at] += jnp.where(lane_c == h - side * (HEADS // 2), both[:, :half] / both[:, half:], 0.0)

    s0[...] = scores(0, 0)
    heads_a_step = HEADS // 4

    def step(n, carry):
        for m in range(heads_a_step):
            one_head(heads_a_step * n + m)

        @pl.when(n == 1)
        def _():
            start_scatter(0, gradient_rows(0))

        @pl.when(n == 2)
        def _():
            start_scatter(1, gradient_rows(1)[: half // 2])
            start_share(0)

        return carry

    lax.fori_loop(0, 4, step, 0)
    start_scatter(2, gradient_rows(1)[half // 2 :])
    start_share(1)
    context = jnp.concatenate([ctx[0], ctx[1]], axis=1).astype(BF16)
    att[...] = (reg[...].astype(F32) + dot(context, wo[...])).astype(BF16)
    pltpu.make_async_copy(att, att_out, att_sem).start()
    start_share(2)
    start_gather(0)
    start_gather(1)
    finish(0, pl.ds(0, half))
    start_gather(2)
    finish(1, pl.ds(half, half // 2))
    finish(2, pl.ds(half + half // 2, half // 2))
    for c, at in enumerate((pl.ds(0, half), pl.ds(half, half // 2), pl.ds(half + half // 2, half // 2))):
        pltpu.make_async_copy(grad.at[at], grad_out.at[at], grad_sems.at[c]).wait()


def layer_kernel(spaces, reps, cap, feat, nb, order, *refs):
    w_hbm, wi_hbm, wo_hbm, cot_hbm, enc_out, att_out, grad_out = refs[:7]
    wi, wo, cot, enc, reg, att, grad, sems = refs[7:15]
    front_refs, attention_refs = refs[15:36], refs[36:]
    v, ctx = attention_refs[3:5]
    loads = [
        pltpu.make_async_copy(source, held, sems.at[n])
        for n, (source, held) in enumerate(((wi_hbm, wi), (wo_hbm, wo), (cot_hbm, cot)))
    ]

    def meanwhile():
        v[:, :, ctx.shape[2] :] = jnp.ones(ctx.shape, BF16)
        ctx[...] = jnp.zeros_like(ctx)

    front_body(spaces, reps, cap, feat, nb, order, w_hbm, enc_out, enc, reg, sems.at[3], loads, meanwhile, *front_refs)
    grad_sems = attention_refs[0]
    attention_body(
        spaces, reps, reg, wi, wo, cot, att_out, att, grad_out, grad, loads, sems.at[4], grad_sems, *attention_refs[1:]
    )
    pltpu.make_async_copy(enc, enc_out, sems.at[3]).wait()
    pltpu.make_async_copy(att, att_out, sems.at[4]).wait()


def layer(features, neighbours, order, weight, wi, wo, cot):
    spaces, reps = lax.axis_size("space"), lax.axis_size("rep")
    rows, width = features.shape
    cap = 3 * rows // (2 * spaces)
    bricks = rows // EDGE**3
    face = EDGE * EDGE
    half = width // 2
    inner, outer = 8, spaces // 8
    planes, others = spaces // 2, 2 * reps
    tile = 256
    vmem = pl.BlockSpec(memory_space=pltpu.VMEM)
    hbm = pl.BlockSpec(memory_space=pl.ANY)
    dma = pltpu.SemaphoreType.DMA
    full = pltpu.VMEM((rows, width), BF16)
    shared = [
        pltpu.VMEM(wi.shape, BF16),
        pltpu.VMEM(wo.shape, BF16),
        *[full] * 4,
        pltpu.VMEM((width, width), F32),
        dma((5,)),
    ]
    for_front = [
        pltpu.VMEM(weight.shape, BF16),
        pltpu.VMEM(((EDGE + 2) * bricks * face, 9 * width), BF16),
        pltpu.VMEM((bricks, face, width), BF16),
        pltpu.VMEM((bricks, face, width), BF16),
        pltpu.VMEM((inner, outer, 8, 128), F32),
        pltpu.VMEM((inner, outer, 8, 128), F32),
        pltpu.VMEM((outer, inner, 8, 128), F32),
        pltpu.VMEM((spaces, cap, width), BF16),
        pltpu.VMEM((spaces, cap, width), BF16),
        pltpu.VMEM((rows, spaces * cap), BF16),
        pltpu.VMEM((spaces * cap, rows), BF16),
        pltpu.VMEM((2, rows // 2, width), F32),
        dma,
        dma((2 * bricks,)),
        dma((2 * bricks,)),
        *[dma((inner,))] * 2,
        *[dma((outer,))] * 2,
        *[dma((spaces,))] * 2,
    ]
    for_attention = [
        dma((3,)),
        full,
        full,
        pltpu.VMEM((2, rows, width), BF16),
        pltpu.VMEM((2, rows, half), F32),
        pltpu.VMEM((tile, rows), F32),
        pltpu.VMEM((tile, rows), F32),
    ]
    for count in (half, half // 2, half // 2):
        for_attention += [
            pltpu.VMEM((others, count // others, width), F32),
            pltpu.VMEM((others, count // others, width), F32),
            pltpu.VMEM((count // others, width), F32),
            pltpu.VMEM((planes, count // others, width), F32),
            pltpu.VMEM((others, count // others, width), F32),
            *[dma((others,))] * 2,
            *[dma((planes,))] * 2,
            *[dma((others,))] * 2,
        ]
    return pl.pallas_call(
        functools.partial(layer_kernel, spaces, reps, cap),
        out_shape=[
            jax.ShapeDtypeStruct((rows, width), BF16),
            jax.ShapeDtypeStruct((rows, width), BF16),
            jax.ShapeDtypeStruct((width, width), F32),
        ],
        in_specs=[vmem, pl.BlockSpec(memory_space=pltpu.SMEM), vmem, hbm, hbm, hbm, hbm],
        out_specs=[hbm] * 3,
        scratch_shapes=shared + for_front + for_attention,
        compiler_params=pltpu.CompilerParams(collective_id=0, has_side_effects=True, vmem_limit_bytes=VMEM_LIMIT),
        cost_estimate=pl.CostEstimate(
            flops=2 * rows * 27 * width * width + 4 * HEADS * rows * rows * width,
            bytes_accessed=weight.size * 2 + 12 * rows * width,
            transcendentals=HEADS * rows * rows,
        ),
        name="layer",
    )(features, neighbours, order, weight, wi, wo, cot)


def publish_kernel(count, *refs):
    given, made, held, sems = refs[:count], refs[count : 2 * count], refs[2 * count : 3 * count], refs[3 * count]
    reads = [pltpu.make_async_copy(given[n], held[n], sems.at[0, n]) for n in range(count)]
    writes = [pltpu.make_async_copy(held[n], made[n], sems.at[1, n]) for n in range(count)]
    for read in reads:
        read.start()
    for read, write in zip(reads, writes):
        read.wait()
        write.start()
    for write in writes:
        write.wait()


def publish(*arrays):
    spec = pl.BlockSpec(memory_space=pl.ANY)
    return pl.pallas_call(
        functools.partial(publish_kernel, len(arrays)),
        out_shape=[jax.ShapeDtypeStruct(a.shape, a.dtype) for a in arrays],
        in_specs=[spec] * len(arrays),
        out_specs=[spec] * len(arrays),
        scratch_shapes=[pltpu.VMEM(a.shape, a.dtype) for a in arrays] + [pltpu.SemaphoreType.DMA((2, len(arrays)))],
        name="publish",
    )(*arrays)


def local(features, neighbours, serial_order, kernel_weight, input_projection, output_projection, cotangent):
    results = layer(
        features[0], neighbours[0], serial_order, kernel_weight, input_projection, output_projection, cotangent[0]
    )
    encoded, attended, gradient = publish(*results)
    return encoded[None], attended[None], gradient


def solution(mesh):
    in_specs = (
        P("rep", "space", None),
        P("rep", "space", None),
        P("rep", "space"),
        P(),
        P(),
        P(),
        P("rep", "space", None),
    )
    out_specs = (P("rep", "space", None), P("rep", "space", None), P())
    return jax.shard_map(local, mesh=mesh, in_specs=in_specs, out_specs=out_specs, check_vma=False)
```
